32 devices in a mesh: band: 2 (over y), xy: 16 (over z, x, core).
Axes of the slice: x: 2, y: 2, z: 4, core: 2. Of those that a mesh axis runs over, the one named last changes fastest.
Arguments:
- orbitals: float32 [4, 16, 128, 256], P('band', 'xy'), may hold values from -6 to 6
- energies: float32 [4], P('band'), may hold values from -1.5 to -0.25
- occupation: int32 [4], P('band'), may hold values from 1 to 2
- potential: float32 [16, 128, 256], P('xy'), may hold values from 0.25 to 2
- trials: float32 [4, 16, 128, 256], P(None, 'xy'), may hold values from -8 to 23
Outputs:
- density: float32 [4, 16, 128, 256], P(None, 'xy', 'band')
- response_matrix: float32 [4, 4], replicated
The draws below stay inside these ranges and needn't reach their ends.
All inputs are finite; a program needn't handle non-finite values.
Results may differ from the reference program's by a relative error of at most 0.0001.
Values sent between devices are 32-bit elements; how exact they have to be, the bound alone decides.
A program may use at most 64 MiB of HBM per device.

```python
import math
import jax
import jax.numpy as jnp
from jax import lax

NY = 128
NZ = 256
K = 4
ITERS = 3
NX = 16
NB = 4


def cosine_rows(frequency, offsets, length):
    positions = jnp.arange(length, dtype=jnp.int32)
    reduced = frequency[..., None] * positions % length
    return jnp.cos(2.0 * math.pi / length * reduced.astype(jnp.float32) + offsets[..., None])


def draw_orbitals(key, part):
    ordering = jax.random.permutation(jax.random.fold_in(key, 3), 64)[:NB]
    freq_x = 1 + ordering % 4
    freq_y = 1 + ordering // 4 % 4
    freq_z = 1 + ordering // 16
    offsets = jax.random.uniform(jax.random.fold_in(key, 5), (3, NB), jnp.float32, 0.0, 2.0 * math.pi)
    along_x = cosine_rows(freq_x, offsets[0], NX)
    along_y = cosine_rows(freq_y, offsets[1], NY)
    along_z = cosine_rows(freq_z, offsets[2], NZ)
    modes = math.sqrt(8.0) * along_x[:, :, None, None] * along_y[:, None, :, None] * along_z[:, None, None, :]
    noise_key = jax.random.fold_in(key, 11)
    noise = 0.5 * jnp.clip(jax.random.normal(noise_key, (NB, NX, NY, NZ), jnp.float32), -6.0, 6.0)
    return (modes + noise).astype(jnp.float32)


def draw_trials(key, part):
    amplitude = 0.4
    frequency = jnp.broadcast_to(jnp.arange(1, 5, dtype=jnp.int32), (K, 4))

    def smooth_factor(index, length):
        weights = jax.random.uniform(jax.random.fold_in(key, 20 + index), (K, 4), jnp.float32, -amplitude, amplitude)
        offsets = jax.random.uniform(jax.random.fold_in(key, 30 + index), (K, 4), jnp.float32, 0.0, 2.0 * math.pi)
        return 1.0 + jnp.sum(weights[:, :, None] * cosine_rows(frequency, offsets, length), axis=1)
    factor_x = smooth_factor(0, NX)
    factor_y = smooth_factor(1, NY)
    factor_z = smooth_factor(2, NZ)
    smooth = factor_x[:, :, None, None] * factor_y[:, None, :, None] * factor_z[:, None, None, :]
    rough_key = jax.random.fold_in(key, 41)
    rough = jax.random.uniform(rough_key, (K, NX, NY, NZ), jnp.float32, -0.5, 0.5)
    return (smooth + rough).astype(jnp.float32)


def place_ends(drawn, own_key, low, largest):
    spot = [jax.random.randint(jax.random.fold_in(own_key, axis), (), 0, length) for axis, length in enumerate(drawn.shape)]
    longest = drawn.shape.index(max(drawn.shape))
    neighbour = spot[:longest] + [(spot[longest] + 1) % drawn.shape[longest]] + spot[longest + 1:]
    return drawn.at[tuple(spot)].set(low).at[tuple(neighbour)].set(largest)


def block_levels(rng, dims, split, low, top_value):
    gain = 1.0
    for dim, shards_of in split:
        steps = jax.random.uniform(jax.random.fold_in(jax.random.fold_in(rng, 6), dim), (shards_of,), jnp.float32, low / len(split), top_value / len(split))
        gain = gain * jnp.repeat(jnp.exp(steps), dims[dim] // shards_of).reshape((-1,) + (1,) * (len(dims) - 1 - dim))
    return gain


def setup_inputs(seed: int = 0) -> dict:
    arg_keys = jax.random.split(jax.random.key(seed), 6)
    orbitals = draw_orbitals(jax.random.fold_in(arg_keys[5], 71), 0)
    energies = jnp.clip(-1.5 + 1.25 * jax.random.uniform(arg_keys[1], (NB,), jnp.float32) ** block_levels(arg_keys[1], (NB,), ((0, 2),), -0.2, 0.2), -1.5, -0.25)
    occupation = place_ends(jax.random.randint(arg_keys[2], (NB,), 1, 3), jax.random.fold_in(arg_keys[2], 1), 1, 2).astype(jnp.int32)
    potential = jnp.clip(0.25 + 1.75 * jax.random.uniform(arg_keys[3], (NX, NY, NZ), jnp.float32) ** block_levels(arg_keys[3], (NX, NY, NZ), ((0, 16),), -0.2, 0.2), 0.25, 2.0)
    trials = draw_trials(jax.random.fold_in(arg_keys[5], 71), 0)
    return dict(orbitals=orbitals, energies=energies, occupation=occupation, potential=potential, trials=trials)


def reference(orbitals, energies, occupation, potential, trials):
    orbital_total = orbitals.shape[0]
    trial_count = trials.shape[0]
    cell_total = potential.size
    grid_shape = potential.shape
    highest = lax.Precision.HIGHEST
    psi_flat = orbitals.reshape(orbital_total, cell_total)
    trial_flat = trials.reshape(trial_count, cell_total)
    potential_flat = potential.reshape(1, cell_total)

    def project(vectors):
        intersection = jnp.dot(psi_flat, vectors.T, precision=highest, preferred_element_type=jnp.float32) / cell_total
        return vectors - jnp.dot(intersection.T, psi_flat, precision=highest, preferred_element_type=jnp.float32)

    def apply_op(vectors, diagonal_op):
        field_block = vectors.reshape((trial_count,) + grid_shape)
        beside = jnp.roll(field_block, 1, 1) + jnp.roll(field_block, -1, 1)
        beside = beside + jnp.roll(field_block, 1, 2) + jnp.roll(field_block, -1, 2)
        z_padded = jnp.pad(field_block, ((0, 0), (0, 0), (0, 0), (1, 1)))
        beside = beside + z_padded[..., 2:] + z_padded[..., :-2]
        return diagonal_op * vectors - 0.5 * beside.reshape(trial_count, cell_total)

    def one_orbital(running, inputs):
        psi_row, energy, weight = inputs
        diagonal_op = 3.0 + potential_flat - energy
        right_side = -project(trial_flat * psi_row[None, :])
        update = project(right_side / diagonal_op)
        for iteration in range(ITERS):
            residual = right_side - apply_op(update, diagonal_op)
            update = update + project(residual / diagonal_op)
        return (running + (weight * psi_row)[None, :] * update, None)
    initial = jnp.zeros((trial_count, cell_total), jnp.float32)
    running, unused = lax.scan(one_orbital, initial, (psi_flat, energies, occupation.astype(jnp.float32)))
    density = running / math.sqrt(orbital_total)
    response_matrix = jnp.dot(density, trial_flat.T, precision=highest, preferred_element_type=jnp.float32) / cell_total
    return (density.reshape((trial_count,) + grid_shape), response_matrix)
```

```python
import functools
import math

import jax
import jax.numpy as jnp
from jax import lax
from jax.experimental import pallas as pl
from jax.experimental.pallas import tpu as pltpu
from jax.sharding import PartitionSpec as P

ITERS = 3
REACH = 2
SLABS = 2 * REACH + 1
MID = REACH
EDGE = 8
HIGHEST = lax.Precision.HIGHEST


def round_up(value, unit):
    return -(-value // unit) * unit


def reduce_groups(bands, slabs):
    groups = []
    stride = 1
    while stride < slabs:
        size = 4 if (slabs // stride) % 4 == 0 else slabs // stride
        groups.append(("xy", size, stride))
        stride *= size
    if bands > 1:
        groups.append(("band", bands, 1))
    return groups


def kernel(dims, groups, orb_ref, energy_ref, occ_ref, pot_ref, trial_ref, dens_ref, resp_ref,
           psi, tri, psi_out, meta, h, u0, v1, v2, lpsi, a_buf, t_out, t_in,
           part, ca, cb, c0f, cf, e0, e1, e2, reds,
           psi_send, psi_recv, tri_send, tri_recv, meta_send, meta_recv, t_send, t_recv,
           red_send, red_recv):
    bands, slabs, nd, kk, ny, nz = dims
    nb = nd * bands
    ys = ny // bands
    ext = ys + 2 * EDGE
    kp, jp = round_up(kk, 8), round_up(nb, 8)
    cells = slabs * ny * nz
    b, p = lax.axis_index("band"), lax.axis_index("xy")

    def at_band(r):
        return lax.rem(b + (r + bands), bands)

    def at_slab(d):
        return lax.rem(p + (d + slabs), slabs)

    def group_rank(g):
        axis, size, stride = groups[g]
        return lax.rem((p if axis == "xy" else b) // stride, size)

    def group_peer(g, q):
        axis, size, stride = groups[g]
        rank = group_rank(g)
        step = (lax.rem(rank + q, size) - rank) * stride
        return {"band": b, "xy": p + step} if axis == "xy" else {"band": b + step, "xy": p}

    barrier = pltpu.get_barrier_semaphore()
    count = 0
    for d in range(-REACH, REACH + 1):
        for r in range(bands):
            if d or r:
                pl.semaphore_signal(barrier, inc=1, device_id={"band": at_band(r), "xy": at_slab(d)},
                                    device_id_type=pl.DeviceIdType.MESH)
                count += 1
    for g, (axis, size, stride) in enumerate(groups):
        for q in range(1, size):
            pl.semaphore_signal(barrier, inc=1, device_id=group_peer(g, q),
                                device_id_type=pl.DeviceIdType.MESH)
            count += 1

    def fill(dst, row_band, src):
        first = pl.multiple_of(row_band * ys, 8)
        low = pl.multiple_of(lax.rem(first + (ny - EDGE), ny), 8)
        high = pl.multiple_of(lax.rem(first + ys, ny), 8)
        dst[0:EDGE, :] = src[pl.ds(low, EDGE), :]
        dst[EDGE:EDGE + ys, :] = src[pl.ds(first, ys), :]
        dst[EDGE + ys:ext, :] = src[pl.ds(high, EDGE), :]

    own = pl.ds(b * nd, nd)
    for l in range(nd):
        fill(psi.at[MID, b * nd + l], b, orb_ref.at[l, 0])
        for r in range(1, bands):
            fill(psi_out.at[r, l], at_band(r), orb_ref.at[l, 0])
    for k in range(kk):
        fill(tri.at[MID, k], b, trial_ref.at[k, 0])
    fill(tri.at[MID, kk], b, pot_ref.at[0])
    for l in range(nd):
        meta[b, l:l + 1, :] = jnp.full((1, nz), energy_ref[l], jnp.float32)
        meta[b, 8 + l:9 + l, :] = jnp.full((1, nz), occ_ref[l].astype(jnp.float32), jnp.float32)

    pl.semaphore_wait(barrier, count)

    def remote(src, dst, send, recv, device):
        return pltpu.make_async_remote_copy(src_ref=src, dst_ref=dst, send_sem=send, recv_sem=recv,
                                            device_id=device, device_id_type=pl.DeviceIdType.MESH)

    def meta_copy(r, from_band):
        return remote(meta.at[b], meta.at[from_band], meta_send.at[r], meta_recv.at[r],
                      {"band": at_band(r), "xy": p})

    def psi_copy(d, r, from_band):
        src = psi.at[MID, own] if r == 0 else psi_out.at[r]
        return remote(src, psi.at[MID - d, pl.ds(from_band * nd, nd)], psi_send.at[d + MID, r],
                      psi_recv.at[MID - d, r], {"band": at_band(r), "xy": at_slab(d)})

    def tri_copy(d):
        return remote(tri.at[MID], tri.at[MID - d], tri_send.at[d + MID], tri_recv.at[MID - d],
                      {"band": b, "xy": at_slab(d)})

    order = [0] + [s * d for d in range(1, REACH + 1) for s in (1, -1)]
    sent = []
    for r in range(1, bands):
        sent.append(meta_copy(r, b))
    for d in order:
        for r in range(bands):
            if d or r:
                sent.append(psi_copy(d, r, b))
        if d:
            sent.append(tri_copy(d))
    for copy in sent:
        copy.start()

    def wait_slab(s):
        d = MID - s
        for r in range(bands):
            if d or r:
                psi_copy(d, r, at_band(-r)).wait_recv()
        if d:
            tri_copy(d).wait_recv()

    lanes = lax.broadcasted_iota(jnp.int32, (ext, nz), 1)

    def around(c):
        return (pltpu.roll(c, 1, 0) + pltpu.roll(c, ext - 1, 0)
                + jnp.where(lanes == 0, 0.0, pltpu.roll(c, 1, 1))
                + jnp.where(lanes == nz - 1, 0.0, pltpu.roll(c, nz - 1, 1)))

    core = slice(EDGE, EDGE + ys)

    def put(row, value):
        folded = jnp.sum(value, axis=0, keepdims=True)
        part[pl.ds(row, 1), :] = sum(folded[:, z:z + 128] for z in range(0, nz, 128))

    def total(which, rows, scale, dst):
        length = round_up(rows, 1024) // 8
        lines = lax.broadcasted_iota(jnp.int32, (8, 128), 0)
        y = jnp.zeros((8, length), jnp.float32)
        for line in range(8):
            y = y + lax.dot_general(jnp.where(lines == line, 1.0, 0.0),
                                    part[line * length:(line + 1) * length, :],
                                    (((1,), (1,)), ((), ())), precision=HIGHEST,
                                    preferred_element_type=jnp.float32)
        for g, (axis, size, stride) in enumerate(groups):
            rank = group_rank(g)
            buf = reds[which * len(groups) + g]
            buf[rank, :, :] = y

            def hop(q, slot):
                return remote(buf.at[rank], buf.at[slot], red_send.at[which, g, q],
                              red_recv.at[which, g, q], group_peer(g, q))

            hops = [hop(q, rank) for q in range(1, size)]
            for copy in hops:
                copy.start()
            for q in range(1, size):
                hop(q, lax.rem(rank + (size - q), size)).wait_recv()
            y = buf[0]
            for slot in range(1, size):
                y = y + buf[slot]
            sent.extend(hops)
        for line in range(8):
            dst[line * length:(line + 1) * length, :] = lax.dot_general(
                y, jnp.where(lines == line, scale, 0.0), (((0,), (0,)), ((), ())),
                precision=HIGHEST, preferred_element_type=jnp.float32)

    def wide(row):
        return jnp.concatenate([row] * (nz // 128), axis=1)

    def energy_row(i):
        return meta[i // nd, pl.ds(i % nd, 1), :]

    def occ_row(i):
        return meta[i // nd, pl.ds(8 + i % nd, 1), :]

    def fill_h(s):
        @pl.loop(0, nb)
        def _(i):
            h[s, i] = 0.5 / (3.0 + tri[s, kk] - energy_row(i))

    for r in range(1, bands):
        meta_copy(r, at_band(-r)).wait_recv()
    wait_slab(MID)
    fill_h(MID)
    block = nb * nb * kp
    square = nb * nb * jp
    part[...] = jnp.zeros_like(part)

    @pl.loop(0, nb)
    def _(i):
        mine = psi[MID, i, core, :]
        inv = 2.0 * h[MID, i, core, :]

        @pl.loop(0, nb)
        def _(j):
            other = psi[MID, j, core, :]
            pair = mine * other
            for k in range(kk):
                both = pair * tri[MID, k, core, :]
                put((i * nb + j) * kp + k, both)
                put(block + (i * nb + j) * kp + k, both * inv)
            weighted = other * inv
            for m in range(nb):
                put(2 * block + (i * nb + j) * jp + m, weighted * psi[MID, m, core, :])
            put(2 * block + square + i * jp + j, pair)

    size_a = 2 * block + square + nb * jp
    total(0, size_a, 1.0 / cells, ca)

    def tile(ref, base, i, j, unit):
        return ref[pl.ds(pl.multiple_of(base + (i * nb + j) * unit, 8), 8), :]

    def apply(ref, base, i, j, vectors):
        return sum(ref[pl.ds(base + (i * nb + j) * jp + m, 1), :] * vectors[m] for m in range(nb))

    def gram(j, vectors):
        base = 2 * block + square + j * jp
        return sum(ca[base + m:base + m + 1, :] * vectors[m] for m in range(nb))

    @pl.loop(0, nb)
    def _(i):
        c0 = [tile(ca, 0, i, j, kp) for j in range(nb)]
        for j in range(nb):
            cf[i, j] = apply(ca, 2 * block, i, j, c0) - tile(ca, block, i, j, kp)
            c0f[i, j] = c0[j]

    def fill_u0(s):
        @pl.loop(0, nb)
        def _(i):
            @pl.loop(0, kk)
            def _(k):
                mine = psi[s, i]
                first = -(tri[s, k] * mine)
                second = jnp.zeros_like(first)
                for j in range(nb):
                    field = psi[s, j]
                    first = first + field * wide(c0f[i, j, pl.ds(k, 1), :])
                    second = second + field * wide(cf[i, j, pl.ds(k, 1), :])
                u0[s, i, k] = 2.0 * h[s, i] * first - second

    fill_u0(MID)
    for s in (MID - 1, MID + 1):
        wait_slab(s)
        fill_h(s)
        fill_u0(s)

    @pl.loop(0, nb)
    def _(j):
        lpsi[j] = psi[MID - 1, j] + psi[MID + 1, j] + around(psi[MID, j])

    part[...] = jnp.zeros_like(part)
    for s in (MID - 2, MID + 2):
        wait_slab(s)
        fill_h(s)
        fill_u0(s)

    @pl.loop(0, nb)
    def _(i):
        @pl.loop(0, nb)
        def _(j):
            a_buf[j] = (h[MID - 1, i] * psi[MID - 1, j] + h[MID + 1, i] * psi[MID + 1, j]
                        + around(h[MID, i] * psi[MID, j]))

        @pl.loop(0, kk)
        def _(k):
            for n, s in enumerate((MID - 1, MID, MID + 1)):
                v1[n] = h[s, i] * (u0[s - 1, i, k] + u0[s + 1, i, k] + around(u0[s, i, k]))
            new = h[MID, i] * (u0[MID - 1, i, k] + v1[0] + u0[MID + 1, i, k] + v1[2]
                               + around(u0[MID, i, k] + v1[1]))
            v2[i, k] = new
            first, second = v1[1, core, :], v2[i, k, core, :]
            for j in range(nb):
                row = (i * nb + j) * kp + k
                put(row, psi[MID, j, core, :] * first)
                put(block + row, psi[MID, j, core, :] * second)
                put(2 * block + row, a_buf[j, core, :] * second)

        @pl.loop(0, nb)
        def _(m):
            seen = h[MID, i, core, :] * lpsi[m, core, :]
            for j in range(nb):
                row = (i * nb + j) * jp + m
                put(3 * block + row, psi[MID, j, core, :] * seen)
                put(3 * block + square + row, a_buf[j, core, :] * seen)

    size_b = 3 * block + 2 * square
    total(1, size_b, 1.0 / cells, cb)

    @pl.loop(0, nb)
    def _(i):
        once = 3 * block
        twice = 3 * block + square
        start = [cf[i, j] for j in range(nb)]
        mu1 = [tile(cb, 0, i, j, kp) for j in range(nb)]
        b0 = [start[j] - gram(j, start) for j in range(nb)]
        x0 = [b0[j] - mu1[j] for j in range(nb)]
        m1 = [tile(cb, block, i, j, kp) + apply(cb, once, i, j, x0) for j in range(nb)]
        x1 = [b0[j] + mu1[j] + gram(j, x0) - m1[j] for j in range(nb)]
        m2 = [mu1[j] + tile(cb, 2 * block, i, j, kp) + apply(cb, twice, i, j, x0)
              + apply(cb, once, i, j, x1) for j in range(nb)]
        for j in range(nb):
            e0[i, j] = x0[j]
            e1[i, j] = x1[j]
            e2[i, j] = b0[j] + m1[j] + gram(j, x1) - m2[j]

    t_out[...] = jnp.zeros_like(t_out)

    @pl.loop(0, nb)
    def _(i):
        weight = occ_row(i)

        @pl.loop(0, kk)
        def _(k):
            first = jnp.zeros((ext, nz), jnp.float32)
            second = u0[MID, i, k] + v2[i, k]
            for j in range(nb):
                first = first + lpsi[j] * wide(e0[i, j, pl.ds(k, 1), :])
                second = second + psi[MID, j] * wide(e1[i, j, pl.ds(k, 1), :])
            v2[i, k] = second + h[MID, i] * first
            inner = v2[i, k, core, :]
            for n, s in enumerate((MID - 1, MID + 1)):
                t_out[n, k] += weight * psi[s, i, core, :] * h[s, i, core, :] * inner

    def t_copy(n):
        return remote(t_out.at[n], t_in.at[n], t_send.at[n], t_recv.at[n],
                      {"band": b, "xy": at_slab(2 * n - 1)})

    for n in range(2):
        t_copy(n).start()
        sent.append(t_copy(n))

    dens_ref[...] = jnp.zeros_like(dens_ref)

    @pl.loop(0, nb)
    def _(i):
        weight = occ_row(i)

        @pl.loop(0, kk)
        def _(k):
            beside = (h[MID, i] * around(v2[i, k]))[core, :]
            flat = u0[MID, i, k, core, :]
            for j in range(nb):
                flat = flat + psi[MID, j, core, :] * wide(e2[i, j, pl.ds(k, 1), :])
            dens_ref[k, 0] += weight * psi[MID, i, core, :] * (flat + beside)

    part[0:1024, :] = jnp.zeros((1024, 128), jnp.float32)

    @pl.loop(0, kk)
    def _(k):
        for l in range(kk):
            put(l * kp + k, tri[MID, l, core, :] * dens_ref[k, 0]
                + tri[MID - 1, l, core, :] * t_out[0, k] + tri[MID + 1, l, core, :] * t_out[1, k])

    scale = 1.0 / math.sqrt(nb)
    total(2, kk * kp, scale / cells, ca)
    column = lax.broadcasted_iota(jnp.int32, (kp, 128), 1)
    picked = sum(jnp.where(column == l, ca[l * kp:(l + 1) * kp, :], 0.0) for l in range(kk))
    resp_ref[...] = picked[:kk, :kk]
    for n in range(2):
        t_copy(n).wait_recv()

    @pl.loop(0, kk)
    def _(k):
        dens_ref[k, 0] = scale * (dens_ref[k, 0] + t_in[0, k] + t_in[1, k])

    for copy in sent:
        copy.wait_send()


def local(sizes, orbitals, energies, occupation, potential, trials):
    bands, slabs = sizes
    nd, width, ny, nz = orbitals.shape
    kk = trials.shape[0]
    nb = nd * bands
    ys = ny // bands
    ext = ys + 2 * EDGE
    kp, jp = round_up(kk, 8), round_up(nb, 8)
    block, square = nb * nb * kp, nb * nb * jp
    rows_a = round_up(2 * block + square + nb * jp, 1024)
    rows_b = round_up(3 * block + 2 * square, 1024)
    rows_c = round_up(kk * kp, 1024)
    groups = reduce_groups(bands, slabs)
    widest = max(size for axis, size, stride in groups)

    def f32(*shape):
        return pltpu.VMEM(shape, jnp.float32)

    dma = pltpu.SemaphoreType.DMA
    scratch = [
        f32(SLABS, nb, ext, nz), f32(SLABS, kk + 1, ext, nz), f32(bands, nd, ext, nz),
        f32(bands, 16, nz), f32(SLABS, nb, ext, nz), f32(SLABS, nb, kk, ext, nz),
        f32(3, ext, nz), f32(nb, kk, ext, nz), f32(nb, ext, nz),
        f32(nb, ext, nz), f32(2, kk, ys, nz), f32(2, kk, ys, nz),
        f32(max(rows_a, rows_b), 128), f32(rows_a, 128), f32(rows_b, 128),
        f32(nb, nb, kp, 128), f32(nb, nb, kp, 128), f32(nb, nb, kp, 128),
        f32(nb, nb, kp, 128), f32(nb, nb, kp, 128),
        [f32(size, 8, rows // 8) for rows in (rows_a, rows_b, rows_c) for axis, size, stride in groups],
        dma((SLABS, bands)), dma((SLABS, bands)), dma((SLABS,)), dma((SLABS,)),
        dma((bands,)), dma((bands,)), dma((2,)), dma((2,)),
        dma((3, len(groups), widest)), dma((3, len(groups), widest)),
    ]
    vmem = pl.BlockSpec(memory_space=pltpu.VMEM)
    smem = pl.BlockSpec(memory_space=pltpu.SMEM)
    return pl.pallas_call(
        functools.partial(kernel, (bands, slabs, nd, kk, ny, nz), groups),
        out_shape=(jax.ShapeDtypeStruct((kk, width, ys, nz), jnp.float32),
                   jax.ShapeDtypeStruct((kk, kk), jnp.float32)),
        in_specs=[vmem, smem, smem, vmem, vmem],
        out_specs=(vmem, vmem),
        scratch_shapes=scratch,
        compiler_params=pltpu.CompilerParams(collective_id=0, has_side_effects=True,
                                             vmem_limit_bytes=56 * 1024 * 1024),
    )(orbitals, energies, occupation, potential, trials)


def solution(mesh):
    in_specs = (
        P("band", "xy", None, None),
        P("band"),
        P("band"),
        P("xy", None, None),
        P(None, "xy", None, None),
    )
    out_specs = (P(None, "xy", "band", None), P())
    sizes = (mesh.shape["band"], mesh.shape["xy"])
    return jax.shard_map(functools.partial(local, sizes), mesh=mesh, in_specs=in_specs,
                         out_specs=out_specs, check_vma=False)
```

```python
import functools
import math

import jax
import jax.numpy as jnp
from jax import lax
from jax.experimental import pallas as pl
from jax.experimental.pallas import tpu as pltpu
from jax.sharding import PartitionSpec as P

ITERS = 3
REACH = 2
SLABS = 2 * REACH + 1
MID = REACH
EDGE = 8
MIDDLE, PARTNER, NEAR, FAR, PASSED = range(5)
HIGHEST = lax.Precision.HIGHEST


def round_up(value, unit):
    return -(-value // unit) * unit


def reduce_groups(bands, slabs):
    groups = []
    stride = 1
    while stride < slabs:
        size = 4 if (slabs // stride) % 4 == 0 else slabs // stride
        groups.append(("xy", size, stride))
        stride *= size
    if bands > 1:
        groups.append(("band", bands, 1))
    return groups


def kernel(dims, groups, orb_ref, energy_ref, occ_ref, pot_ref, trial_ref, dens_ref, resp_ref,
           psi, tri, psi_out, meta, h, u0, v1, v2, lpsi, a_buf, t_out, t_in,
           part, ca, cb, c0f, cf, e0, e1, e2, reds,
           psi_send, psi_recv, tri_send, tri_recv, meta_send, meta_recv, t_send, t_recv,
           red_send, red_recv):
    bands, slabs, nd, kk, ny, nz = dims
    nb = nd * bands
    ys = ny // bands
    ext = ys + EDGE
    kp, jp = round_up(kk, 8), round_up(nb, 8)
    cells = slabs * ny * nz
    b, p = lax.axis_index("band"), lax.axis_index("xy")

    out = 2 * lax.rem(p, 2) - 1

    def at_band(r):
        return lax.rem(b + (r + bands), bands)

    def at_slab(d):
        return lax.rem(p + (d + slabs), slabs)

    def group_rank(g):
        axis, size, stride = groups[g]
        return lax.rem((p if axis == "xy" else b) // stride, size)

    def group_peer(g, q):
        axis, size, stride = groups[g]
        rank = group_rank(g)
        step = (lax.rem(rank + q, size) - rank) * stride
        return {"band": b, "xy": p + step} if axis == "xy" else {"band": b + step, "xy": p}

    barrier = pltpu.get_barrier_semaphore()
    count = 0
    for d in range(-REACH, REACH + 1):
        for r in range(bands):
            if d or r:
                pl.semaphore_signal(barrier, inc=1, device_id={"band": at_band(r), "xy": at_slab(d)},
                                    device_id_type=pl.DeviceIdType.MESH)
                count += 1
    for g, (axis, size, stride) in enumerate(groups):
        for q in range(1, size):
            pl.semaphore_signal(barrier, inc=1, device_id=group_peer(g, q),
                                device_id_type=pl.DeviceIdType.MESH)
            count += 1

    def fill(dst, row_band, src):
        first = pl.multiple_of(row_band * ys, 8)
        low = pl.multiple_of(lax.rem(first + (ny - EDGE), ny), 8)
        high = pl.multiple_of(lax.rem(first + ys, ny), 8)
        dst[0:ys, :] = src[pl.ds(first, ys), :]
        dst[ys:ext, :] = jnp.where(lax.broadcasted_iota(jnp.int32, (EDGE, nz), 0) < EDGE // 2,
                                   src[pl.ds(high, EDGE), :], src[pl.ds(low, EDGE), :])

    own = pl.ds(b * nd, nd)
    for l in range(nd):
        fill(psi.at[MID, b * nd + l], b, orb_ref.at[l, 0])
        for r in range(1, bands):
            fill(psi_out.at[r, l], at_band(r), orb_ref.at[l, 0])
    for k in range(kk):
        fill(tri.at[MID, k], b, trial_ref.at[k, 0])
    fill(tri.at[MID, kk], b, pot_ref.at[0])
    for l in range(nd):
        meta[b, l:l + 1, :] = jnp.full((1, nz), energy_ref[l], jnp.float32)
        meta[b, 8 + l:9 + l, :] = jnp.full((1, nz), occ_ref[l].astype(jnp.float32), jnp.float32)

    pl.semaphore_wait(barrier, count)

    def remote(src, dst, send, recv, device):
        return pltpu.make_async_remote_copy(src_ref=src, dst_ref=dst, send_sem=send, recv_sem=recv,
                                            device_id=device, device_id_type=pl.DeviceIdType.MESH)

    def meta_copy(r, from_band):
        return remote(meta.at[b], meta.at[from_band], meta_send.at[r], meta_recv.at[r],
                      {"band": at_band(r), "xy": p})

    def place(role):
        return {MIDDLE: (0, MID), PARTNER: (-out, MID + out), NEAR: (out, MID - out),
                FAR: (-2 * out, MID + 2 * out), PASSED: (-out, MID + 2 * out)}[role]

    def psi_copy(role, r, first, count):
        d, slot = place(role)
        if role == PASSED:
            src = psi.at[MID + out, :]
        elif r == 0:
            src = psi.at[MID, own]
        elif role == MIDDLE:
            src = psi_out.at[r]
        else:
            src = psi_out.at[r, :]
        dst = psi.at[slot, pl.ds(first, count)]
        if role != MIDDLE:
            dst = psi.at[slot, pl.ds(first, count)]
        return remote(src, dst, psi_send.at[role, r], psi_recv.at[role, r],
                      {"band": at_band(r), "xy": at_slab(d)})

    def tri_copy(role):
        d, slot = place(role)
        src = tri.at[MID + out if role == PASSED else MID, :]
        return remote(src, tri.at[slot, :], tri_send.at[role], tri_recv.at[role],
                      {"band": b, "xy": at_slab(d)})

    def copies(role):
        if role == PASSED:
            return [psi_copy(role, 0, 0, nb), tri_copy(role)]
        moved = [psi_copy(role, r, b * nd, nd) for r in range(bands) if r or role != MIDDLE]
        return moved if role == MIDDLE else moved + [tri_copy(role)]

    sent = []

    def send(role):
        for copy in copies(role):
            copy.start()
            sent.append(copy)

    def wait(role):
        if role == PASSED:
            for copy in copies(role):
                copy.wait_recv()
            return
        for r in range(bands):
            if r or role != MIDDLE:
                psi_copy(role, r, at_band(-r) * nd, nd).wait_recv()
        if role != MIDDLE:
            tri_copy(role).wait_recv()

    for r in range(1, bands):
        meta_copy(r, b).start()
        sent.append(meta_copy(r, b))
    send(MIDDLE)
    send(PARTNER)
    send(NEAR)

    lanes = lax.broadcasted_iota(jnp.int32, (ext, nz), 1)

    def around(c):
        return (pltpu.roll(c, 1, 0) + pltpu.roll(c, ext - 1, 0)
                + jnp.where(lanes == 0, 0.0, pltpu.roll(c, 1, 1))
                + jnp.where(lanes == nz - 1, 0.0, pltpu.roll(c, nz - 1, 1)))

    core = slice(0, ys)

    def put(row, value):
        folded = jnp.sum(value, axis=0, keepdims=True)
        part[pl.ds(row, 1), :] = sum(folded[:, z:z + 128] for z in range(0, nz, 128))

    def total(which, rows, scale, dst):
        length = round_up(rows, 1024) // 8
        lines = lax.broadcasted_iota(jnp.int32, (8, 128), 0)
        y = jnp.zeros((8, length), jnp.float32)
        for line in range(8):
            y = y + lax.dot_general(jnp.where(lines == line, 1.0, 0.0),
                                    part[line * length:(line + 1) * length, :],
                                    (((1,), (1,)), ((), ())), precision=HIGHEST,
                                    preferred_element_type=jnp.float32)
        for g, (axis, size, stride) in enumerate(groups):
            rank = group_rank(g)
            buf = reds[which * len(groups) + g]
            buf[rank, :, :] = y

            def hop(q, slot):
                return remote(buf.at[rank], buf.at[slot], red_send.at[which, g, q],
                              red_recv.at[which, g, q], group_peer(g, q))

            hops = [hop(q, rank) for q in range(1, size)]
            for copy in hops:
                copy.start()
            for q in range(1, size):
                hop(q, lax.rem(rank + (size - q), size)).wait_recv()
            y = buf[0]
            for slot in range(1, size):
                y = y + buf[slot]
            sent.extend(hops)
        for line in range(8):
            dst[line * length:(line + 1) * length, :] = lax.dot_general(
                y, jnp.where(lines == line, scale, 0.0), (((0,), (0,)), ((), ())),
                precision=HIGHEST, preferred_element_type=jnp.float32)

    def wide(row):
        return jnp.concatenate([row] * (nz // 128), axis=1)

    def energy_row(i):
        return meta[i // nd, pl.ds(i % nd, 1), :]

    def occ_row(i):
        return meta[i // nd, pl.ds(8 + i % nd, 1), :]

    def fill_h(s):
        @pl.loop(0, nb)
        def _(i):
            h[s, i] = 0.5 / (3.0 + tri[s, kk] - energy_row(i))

    for r in range(1, bands):
        meta_copy(r, at_band(-r)).wait_recv()
    wait(MIDDLE)
    fill_h(MID)
    block = nb * nb * kp
    square = nb * nb * jp
    part[...] = jnp.zeros_like(part)

    @pl.loop(0, nb)
    def _(i):
        mine = psi[MID, i, core, :]
        inv = 2.0 * h[MID, i, core, :]

        @pl.loop(0, nb)
        def _(j):
            other = psi[MID, j, core, :]
            pair = mine * other
            for k in range(kk):
                both = pair * tri[MID, k, core, :]
                put((i * nb + j) * kp + k, both)
                put(block + (i * nb + j) * kp + k, both * inv)
            weighted = other * inv
            for m in range(nb):
                put(2 * block + (i * nb + j) * jp + m, weighted * psi[MID, m, core, :])
            put(2 * block + square + i * jp + j, pair)

    size_a = 2 * block + square + nb * jp
    total(0, size_a, 1.0 / cells, ca)
    send(FAR)

    def tile(ref, base, i, j, unit):
        return ref[pl.ds(pl.multiple_of(base + (i * nb + j) * unit, 8), 8), :]

    def apply(ref, base, i, j, vectors):
        return sum(ref[pl.ds(base + (i * nb + j) * jp + m, 1), :] * vectors[m] for m in range(nb))

    def gram(j, vectors):
        base = 2 * block + square + j * jp
        return sum(ca[base + m:base + m + 1, :] * vectors[m] for m in range(nb))

    @pl.loop(0, nb)
    def _(i):
        c0 = [tile(ca, 0, i, j, kp) for j in range(nb)]
        for j in range(nb):
            cf[i, j] = apply(ca, 2 * block, i, j, c0) - tile(ca, block, i, j, kp)
            c0f[i, j] = c0[j]

    def fill_u0(s):
        @pl.loop(0, nb)
        def _(i):
            @pl.loop(0, kk)
            def _(k):
                mine = psi[s, i]
                first = -(tri[s, k] * mine)
                second = jnp.zeros_like(first)
                for j in range(nb):
                    field = psi[s, j]
                    first = first + field * wide(c0f[i, j, pl.ds(k, 1), :])
                    second = second + field * wide(cf[i, j, pl.ds(k, 1), :])
                u0[s, i, k] = 2.0 * h[s, i] * first - second

    fill_u0(MID)
    wait(PARTNER)
    fill_h(MID - out)
    fill_u0(MID - out)
    wait(NEAR)
    send(PASSED)
    fill_h(MID + out)
    fill_u0(MID + out)

    part[...] = jnp.zeros_like(part)

    @pl.loop(0, nb)
    def _(j):
        lpsi[j] = psi[MID - 1, j] + psi[MID + 1, j] + around(psi[MID, j])

    @pl.loop(0, nb)
    def _(i):
        @pl.loop(0, nb)
        def _(j):
            a_buf[i, j] = (h[MID - 1, i] * psi[MID - 1, j] + h[MID + 1, i] * psi[MID + 1, j]
                           + around(h[MID, i] * psi[MID, j]))[core, :]

        @pl.loop(0, nb)
        def _(m):
            seen = h[MID, i, core, :] * lpsi[m, core, :]
            for j in range(nb):
                row = (i * nb + j) * jp + m
                put(3 * block + row, psi[MID, j, core, :] * seen)
                put(3 * block + square + row, a_buf[i, j] * seen)

        @pl.loop(0, kk)
        def _(k):
            v2[i, k] = h[MID, i] * (u0[MID - 1, i, k] + u0[MID + 1, i, k] + around(u0[MID, i, k]))
            first = v2[i, k, core, :]
            for j in range(nb):
                put((i * nb + j) * kp + k, psi[MID, j, core, :] * first)

    wait(FAR)
    fill_h(MID + 2 * out)
    fill_u0(MID + 2 * out)
    wait(PASSED)
    fill_h(MID - 2 * out)
    fill_u0(MID - 2 * out)

    @pl.loop(0, nb)
    def _(i):
        @pl.loop(0, kk)
        def _(k):
            for n, s in enumerate((MID - 1, MID + 1)):
                v1[n] = u0[s, i, k] + h[s, i] * (u0[s - 1, i, k] + u0[s + 1, i, k]
                                                + around(u0[s, i, k]))
            v2[i, k] = h[MID, i] * (v1[0] + v1[1] + around(u0[MID, i, k] + v2[i, k]))
            second = v2[i, k, core, :]
            for j in range(nb):
                row = (i * nb + j) * kp + k
                put(block + row, psi[MID, j, core, :] * second)
                put(2 * block + row, a_buf[i, j] * second)

    size_b = 3 * block + 2 * square
    total(1, size_b, 1.0 / cells, cb)

    @pl.loop(0, nb)
    def _(i):
        once = 3 * block
        twice = 3 * block + square
        start = [cf[i, j] for j in range(nb)]
        mu1 = [tile(cb, 0, i, j, kp) for j in range(nb)]
        b0 = [start[j] - gram(j, start) for j in range(nb)]
        x0 = [b0[j] - mu1[j] for j in range(nb)]
        m1 = [tile(cb, block, i, j, kp) + apply(cb, once, i, j, x0) for j in range(nb)]
        x1 = [b0[j] + mu1[j] + gram(j, x0) - m1[j] for j in range(nb)]
        m2 = [mu1[j] + tile(cb, 2 * block, i, j, kp) + apply(cb, twice, i, j, x0)
              + apply(cb, once, i, j, x1) for j in range(nb)]
        for j in range(nb):
            e0[i, j] = x0[j]
            e1[i, j] = x1[j]
            e2[i, j] = b0[j] + m1[j] + gram(j, x1) - m2[j]

    t_out[...] = jnp.zeros_like(t_out)

    @pl.loop(0, nb)
    def _(i):
        weight = occ_row(i)

        @pl.loop(0, kk)
        def _(k):
            first = jnp.zeros((ext, nz), jnp.float32)
            second = u0[MID, i, k] + v2[i, k]
            for j in range(nb):
                first = first + lpsi[j] * wide(e0[i, j, pl.ds(k, 1), :])
                second = second + psi[MID, j] * wide(e1[i, j, pl.ds(k, 1), :])
            v2[i, k] = second + h[MID, i] * first
            inner = v2[i, k, core, :]
            for n, s in enumerate((MID - 1, MID + 1)):
                t_out[n, k] += weight * psi[s, i, core, :] * h[s, i, core, :] * inner

    def t_copy(n):
        return remote(t_out.at[n], t_in.at[n], t_send.at[n], t_recv.at[n],
                      {"band": b, "xy": at_slab(2 * n - 1)})

    for n in range(2):
        t_copy(n).start()
        sent.append(t_copy(n))

    dens_ref[...] = jnp.zeros_like(dens_ref)

    @pl.loop(0, nb)
    def _(i):
        weight = occ_row(i)

        @pl.loop(0, kk)
        def _(k):
            beside = (h[MID, i] * around(v2[i, k]))[core, :]
            flat = u0[MID, i, k, core, :]
            for j in range(nb):
                flat = flat + psi[MID, j, core, :] * wide(e2[i, j, pl.ds(k, 1), :])
            dens_ref[k, 0] += weight * psi[MID, i, core, :] * (flat + beside)

    part[0:1024, :] = jnp.zeros((1024, 128), jnp.float32)

    @pl.loop(0, kk)
    def _(k):
        for l in range(kk):
            put(l * kp + k, tri[MID, l, core, :] * dens_ref[k, 0]
                + tri[MID - 1, l, core, :] * t_out[0, k] + tri[MID + 1, l, core, :] * t_out[1, k])

    scale = 1.0 / math.sqrt(nb)
    total(2, kk * kp, scale / cells, ca)
    column = lax.broadcasted_iota(jnp.int32, (kp, 128), 1)
    picked = sum(jnp.where(column == l, ca[l * kp:(l + 1) * kp, :], 0.0) for l in range(kk))
    resp_ref[...] = picked[:kk, :kk]
    for n in range(2):
        t_copy(n).wait_recv()

    @pl.loop(0, kk)
    def _(k):
        dens_ref[k, 0] = scale * (dens_ref[k, 0] + t_in[0, k] + t_in[1, k])

    for copy in sent:
        copy.wait_send()


def local(sizes, orbitals, energies, occupation, potential, trials):
    bands, slabs = sizes
    nd, width, ny, nz = orbitals.shape
    kk = trials.shape[0]
    nb = nd * bands
    ys = ny // bands
    ext = ys + EDGE
    kp, jp = round_up(kk, 8), round_up(nb, 8)
    block, square = nb * nb * kp, nb * nb * jp
    rows_a = round_up(2 * block + square + nb * jp, 1024)
    rows_b = round_up(3 * block + 2 * square, 1024)
    rows_c = round_up(kk * kp, 1024)
    groups = reduce_groups(bands, slabs)
    widest = max(size for axis, size, stride in groups)

    def f32(*shape):
        return pltpu.VMEM(shape, jnp.float32)

    dma = pltpu.SemaphoreType.DMA
    scratch = [
        f32(SLABS, nb, ext, nz), f32(SLABS, kk + 1, ext, nz), f32(bands, nd, ext, nz),
        f32(bands, 16, nz), f32(SLABS, nb, ext, nz), f32(SLABS, nb, kk, ext, nz),
        f32(2, ext, nz), f32(nb, kk, ext, nz), f32(nb, ext, nz),
        f32(nb, nb, ys, nz), f32(2, kk, ys, nz), f32(2, kk, ys, nz),
        f32(max(rows_a, rows_b), 128), f32(rows_a, 128), f32(rows_b, 128),
        f32(nb, nb, kp, 128), f32(nb, nb, kp, 128), f32(nb, nb, kp, 128),
        f32(nb, nb, kp, 128), f32(nb, nb, kp, 128),
        [f32(size, 8, rows // 8) for rows in (rows_a, rows_b, rows_c) for axis, size, stride in groups],
        dma((5, bands)), dma((5, bands)), dma((5,)), dma((5,)),
        dma((bands,)), dma((bands,)), dma((2,)), dma((2,)),
        dma((3, len(groups), widest)), dma((3, len(groups), widest)),
    ]
    vmem = pl.BlockSpec(memory_space=pltpu.VMEM)
    smem = pl.BlockSpec(memory_space=pltpu.SMEM)
    return pl.pallas_call(
        functools.partial(kernel, (bands, slabs, nd, kk, ny, nz), groups),
        out_shape=(jax.ShapeDtypeStruct((kk, width, ys, nz), jnp.float32),
                   jax.ShapeDtypeStruct((kk, kk), jnp.float32)),
        in_specs=[vmem, smem, smem, vmem, vmem],
        out_specs=(vmem, vmem),
        scratch_shapes=scratch,
        compiler_params=pltpu.CompilerParams(collective_id=0, has_side_effects=True,
                                             vmem_limit_bytes=56 * 1024 * 1024),
    )(orbitals, energies, occupation, potential, trials)


def solution(mesh):
    in_specs = (
        P("band", "xy", None, None),
        P("band"),
        P("band"),
        P("xy", None, None),
        P(None, "xy", None, None),
    )
    out_specs = (P(None, "xy", "band", None), P())
    sizes = (mesh.shape["band"], mesh.shape["xy"])
    return jax.shard_map(functools.partial(local, sizes), mesh=mesh, in_specs=in_specs,
                         out_specs=out_specs, check_vma=False)
```

```python
import functools
import math

import jax
import jax.numpy as jnp
from jax import lax
from jax.experimental import pallas as pl
from jax.experimental.pallas import tpu as pltpu
from jax.sharding import PartitionSpec as P

ITERS = 3
REACH = 2
SLABS = 2 * REACH + 1
MID = REACH
EDGE = 8
MIDDLE, PARTNER, NEAR, FAR, PASSED = range(5)
HIGHEST = lax.Precision.HIGHEST


def round_up(value, unit):
    return -(-value // unit) * unit


def reduce_groups(bands, slabs):
    groups = []
    stride = 1
    while stride < slabs:
        size = 4 if (slabs // stride) % 4 == 0 else slabs // stride
        groups.append((1 if groups else bands, size, stride))
        stride *= size
    return groups


def message(rows):
    lines = min(8, -(-rows // 128))
    return lines, round_up(-(-rows // lines), 128)


def kernel(dims, groups, orb_ref, energy_ref, occ_ref, pot_ref, trial_ref, dens_ref, resp_ref,
           psi, tri, psi_out, meta, h, u0, v1, v2, lpsi, a_buf, t_out, t_in,
           part, ca, cb, c0f, cf, e0, e1, e2, reds,
           psi_send, psi_recv, tri_send, tri_recv, meta_send, meta_recv, t_send, t_recv,
           red_send, red_recv):
    bands, slabs, nd, kk, ny, nz = dims
    nb = nd * bands
    ys = ny // bands
    ext = ys + EDGE
    kp, jp = round_up(kk, 8), round_up(nb, 8)
    cells = slabs * ny * nz
    b, p = lax.axis_index("band"), lax.axis_index("xy")

    out = 2 * lax.rem(p, 2) - 1

    def at_band(r):
        return lax.rem(b + (r + bands), bands)

    def at_slab(d):
        return lax.rem(p + (d + slabs), slabs)

    def group_size(g):
        return groups[g][0] * groups[g][1]

    def group_rank(g):
        across, size, stride = groups[g]
        rank = lax.rem(p // stride, size)
        return rank + b * size if across > 1 else rank

    def group_peer(g, q):
        across, size, stride = groups[g]
        peer = lax.rem(group_rank(g) + q, group_size(g))
        step = (lax.rem(peer, size) - lax.rem(p // stride, size)) * stride
        return {"band": peer // size if across > 1 else b, "xy": p + step}

    barrier = pltpu.get_barrier_semaphore()
    count = 0
    for d in range(-REACH, REACH + 1):
        for r in range(bands):
            if d or r:
                pl.semaphore_signal(barrier, inc=1, device_id={"band": at_band(r), "xy": at_slab(d)},
                                    device_id_type=pl.DeviceIdType.MESH)
                count += 1
    for g in range(len(groups)):
        for q in range(1, group_size(g)):
            pl.semaphore_signal(barrier, inc=1, device_id=group_peer(g, q),
                                device_id_type=pl.DeviceIdType.MESH)
            count += 1

    def fill(dst, row_band, src):
        first = pl.multiple_of(row_band * ys, 8)
        low = pl.multiple_of(lax.rem(first + (ny - EDGE), ny), 8)
        high = pl.multiple_of(lax.rem(first + ys, ny), 8)
        dst[0:ys, :] = src[pl.ds(first, ys), :]
        dst[ys:ext, :] = jnp.where(lax.broadcasted_iota(jnp.int32, (EDGE, nz), 0) < EDGE // 2,
                                   src[pl.ds(high, EDGE), :], src[pl.ds(low, EDGE), :])

    own = pl.ds(b * nd, nd)
    for l in range(nd):
        fill(psi.at[MID, b * nd + l], b, orb_ref.at[l, 0])
        for r in range(1, bands):
            fill(psi_out.at[r, l], at_band(r), orb_ref.at[l, 0])
    for k in range(kk):
        fill(tri.at[MID, k], b, trial_ref.at[k, 0])
    fill(tri.at[MID, kk], b, pot_ref.at[0])
    for l in range(nd):
        meta[b, l:l + 1, :] = jnp.full((1, nz), energy_ref[l], jnp.float32)
        meta[b, 8 + l:9 + l, :] = jnp.full((1, nz), occ_ref[l].astype(jnp.float32), jnp.float32)

    pl.semaphore_wait(barrier, count)

    def remote(src, dst, send, recv, device):
        return pltpu.make_async_remote_copy(src_ref=src, dst_ref=dst, send_sem=send, recv_sem=recv,
                                            device_id=device, device_id_type=pl.DeviceIdType.MESH)

    def meta_copy(r, from_band):
        return remote(meta.at[b], meta.at[from_band], meta_send.at[r], meta_recv.at[r],
                      {"band": at_band(r), "xy": p})

    def place(role):
        return {MIDDLE: (0, MID), PARTNER: (-out, MID + out), NEAR: (out, MID - out),
                FAR: (-2 * out, MID + 2 * out), PASSED: (-out, MID + 2 * out)}[role]

    def psi_copy(role, r, first, count):
        d, slot = place(role)
        if role == PASSED:
            src = psi.at[MID + out, :]
        elif r == 0:
            src = psi.at[MID, own]
        elif role == MIDDLE:
            src = psi_out.at[r]
        else:
            src = psi_out.at[r, :]
        dst = psi.at[slot, pl.ds(first, count)]
        if role != MIDDLE:
            dst = psi.at[slot, pl.ds(first, count)]
        return remote(src, dst, psi_send.at[role, r], psi_recv.at[role, r],
                      {"band": at_band(r), "xy": at_slab(d)})

    def tri_copy(role):
        d, slot = place(role)
        src = tri.at[MID + out if role == PASSED else MID, :]
        return remote(src, tri.at[slot, :], tri_send.at[role], tri_recv.at[role],
                      {"band": b, "xy": at_slab(d)})

    def copies(role):
        if role == PASSED:
            return [psi_copy(role, 0, 0, nb), tri_copy(role)]
        moved = [psi_copy(role, r, b * nd, nd) for r in range(bands) if r or role != MIDDLE]
        return moved if role == MIDDLE else moved + [tri_copy(role)]

    sent = []

    def send(role):
        for copy in copies(role):
            copy.start()
            sent.append(copy)

    def wait(role):
        if role == PASSED:
            for copy in copies(role):
                copy.wait_recv()
            return
        for r in range(bands):
            if r or role != MIDDLE:
                psi_copy(role, r, at_band(-r) * nd, nd).wait_recv()
        if role != MIDDLE:
            tri_copy(role).wait_recv()

    for r in range(1, bands):
        meta_copy(r, b).start()
        sent.append(meta_copy(r, b))
    send(MIDDLE)
    send(PARTNER)
    send(NEAR)

    lanes = lax.broadcasted_iota(jnp.int32, (ext, nz), 1)

    def around(c):
        return (pltpu.roll(c, 1, 0) + pltpu.roll(c, ext - 1, 0)
                + jnp.where(lanes == 0, 0.0, pltpu.roll(c, 1, 1))
                + jnp.where(lanes == nz - 1, 0.0, pltpu.roll(c, nz - 1, 1)))

    core = slice(0, ys)

    def put(row, value):
        folded = jnp.sum(value, axis=0, keepdims=True)
        part[pl.ds(row, 1), :] = sum(folded[:, z:z + 128] for z in range(0, nz, 128))

    def total(which, rows, scale, dst):
        count, length = message(rows)
        lines = lax.broadcasted_iota(jnp.int32, (8, 128), 0)
        y = jnp.zeros((8, length), jnp.float32)
        for line in range(count):
            y = y + lax.dot_general(jnp.where(lines == line, 1.0, 0.0),
                                    part[line * length:(line + 1) * length, :],
                                    (((1,), (1,)), ((), ())), precision=HIGHEST,
                                    preferred_element_type=jnp.float32)
        for g in range(len(groups)):
            rank, size = group_rank(g), group_size(g)
            buf = reds[which * len(groups) + g]
            buf[rank, :, :] = y

            def hop(q, slot):
                return remote(buf.at[rank], buf.at[slot], red_send.at[which, g, q],
                              red_recv.at[which, g, q], group_peer(g, q))

            hops = [hop(q, rank) for q in range(1, size)]
            for copy in hops:
                copy.start()
            for q in range(1, size):
                hop(q, lax.rem(rank + (size - q), size)).wait_recv()
            y = buf[0]
            for slot in range(1, size):
                y = y + buf[slot]
            sent.extend(hops)
        for line in range(count):
            dst[line * length:(line + 1) * length, :] = lax.dot_general(
                y, jnp.where(lines == line, scale, 0.0), (((0,), (0,)), ((), ())),
                precision=HIGHEST, preferred_element_type=jnp.float32)

    def wide(row):
        return jnp.concatenate([row] * (nz // 128), axis=1)

    def energy_row(i):
        return meta[i // nd, pl.ds(i % nd, 1), :]

    def occ_row(i):
        return meta[i // nd, pl.ds(8 + i % nd, 1), :]

    def fill_h(s):
        @pl.loop(0, nb)
        def _(i):
            h[s, i] = 0.5 / (3.0 + tri[s, kk] - energy_row(i))

    for r in range(1, bands):
        meta_copy(r, at_band(-r)).wait_recv()
    wait(MIDDLE)
    fill_h(MID)
    block = nb * nb * kp
    square = nb * nb * jp
    part[...] = jnp.zeros_like(part)

    @pl.loop(0, nb)
    def _(i):
        mine = psi[MID, i, core, :]
        inv = 2.0 * h[MID, i, core, :]

        @pl.loop(0, nb)
        def _(j):
            other = psi[MID, j, core, :]
            pair = mine * other
            for k in range(kk):
                both = pair * tri[MID, k, core, :]
                put((i * nb + j) * kp + k, both)
                put(block + (i * nb + j) * kp + k, both * inv)
            weighted = other * inv
            for m in range(nb):
                put(2 * block + (i * nb + j) * jp + m, weighted * psi[MID, m, core, :])
            put(2 * block + square + i * jp + j, pair)

    size_a = 2 * block + square + nb * jp
    total(0, size_a, 1.0 / cells, ca)
    send(FAR)

    def tile(ref, base, i, j, unit):
        return ref[pl.ds(pl.multiple_of(base + (i * nb + j) * unit, 8), 8), :]

    def apply(ref, base, i, j, vectors):
        return sum(ref[pl.ds(base + (i * nb + j) * jp + m, 1), :] * vectors[m] for m in range(nb))

    def gram(j, vectors):
        base = 2 * block + square + j * jp
        return sum(ca[base + m:base + m + 1, :] * vectors[m] for m in range(nb))

    @pl.loop(0, nb)
    def _(i):
        c0 = [tile(ca, 0, i, j, kp) for j in range(nb)]
        for j in range(nb):
            cf[i, j] = apply(ca, 2 * block, i, j, c0) - tile(ca, block, i, j, kp)
            c0f[i, j] = c0[j]

    def fill_u0(s):
        @pl.loop(0, nb)
        def _(i):
            @pl.loop(0, kk)
            def _(k):
                mine = psi[s, i]
                first = -(tri[s, k] * mine)
                second = jnp.zeros_like(first)
                for j in range(nb):
                    field = psi[s, j]
                    first = first + field * wide(c0f[i, j, pl.ds(k, 1), :])
                    second = second + field * wide(cf[i, j, pl.ds(k, 1), :])
                u0[s, i, k] = 2.0 * h[s, i] * first - second

    fill_u0(MID)
    wait(PARTNER)
    fill_h(MID - out)
    fill_u0(MID - out)
    wait(NEAR)
    send(PASSED)
    fill_h(MID + out)
    fill_u0(MID + out)

    part[...] = jnp.zeros_like(part)

    @pl.loop(0, nb)
    def _(j):
        lpsi[j] = psi[MID - 1, j] + psi[MID + 1, j] + around(psi[MID, j])

    @pl.loop(0, nb)
    def _(i):
        @pl.loop(0, nb)
        def _(j):
            a_buf[i, j] = (h[MID - 1, i] * psi[MID - 1, j] + h[MID + 1, i] * psi[MID + 1, j]
                           + around(h[MID, i] * psi[MID, j]))[core, :]

        @pl.loop(0, nb)
        def _(m):
            seen = h[MID, i, core, :] * lpsi[m, core, :]
            for j in range(nb):
                row = (i * nb + j) * jp + m
                put(3 * block + row, psi[MID, j, core, :] * seen)
                put(3 * block + square + row, a_buf[i, j] * seen)

        @pl.loop(0, kk, unroll=True)
        def _(k):
            v2[i, k] = h[MID, i] * (u0[MID - 1, i, k] + u0[MID + 1, i, k] + around(u0[MID, i, k]))
            first = v2[i, k, core, :]
            for j in range(nb):
                put((i * nb + j) * kp + k, psi[MID, j, core, :] * first)

    wait(FAR)
    fill_h(MID + 2 * out)
    fill_u0(MID + 2 * out)
    wait(PASSED)
    fill_h(MID - 2 * out)
    fill_u0(MID - 2 * out)

    @pl.loop(0, nb)
    def _(i):
        @pl.loop(0, kk, unroll=True)
        def _(k):
            for n, s in enumerate((MID - 1, MID + 1)):
                v1[n] = u0[s, i, k] + h[s, i] * (u0[s - 1, i, k] + u0[s + 1, i, k]
                                                + around(u0[s, i, k]))
            v2[i, k] = h[MID, i] * (v1[0] + v1[1] + around(u0[MID, i, k] + v2[i, k]))
            second = v2[i, k, core, :]
            for j in range(nb):
                row = (i * nb + j) * kp + k
                put(block + row, psi[MID, j, core, :] * second)
                put(2 * block + row, a_buf[i, j] * second)

    size_b = 3 * block + 2 * square
    total(1, size_b, 1.0 / cells, cb)

    @pl.loop(0, nb)
    def _(i):
        once = 3 * block
        twice = 3 * block + square
        start = [cf[i, j] for j in range(nb)]
        mu1 = [tile(cb, 0, i, j, kp) for j in range(nb)]
        b0 = [start[j] - gram(j, start) for j in range(nb)]
        x0 = [b0[j] - mu1[j] for j in range(nb)]
        m1 = [tile(cb, block, i, j, kp) + apply(cb, once, i, j, x0) for j in range(nb)]
        x1 = [b0[j] + mu1[j] + gram(j, x0) - m1[j] for j in range(nb)]
        m2 = [mu1[j] + tile(cb, 2 * block, i, j, kp) + apply(cb, twice, i, j, x0)
              + apply(cb, once, i, j, x1) for j in range(nb)]
        for j in range(nb):
            e0[i, j] = x0[j]
            e1[i, j] = x1[j]
            e2[i, j] = b0[j] + m1[j] + gram(j, x1) - m2[j]

    t_out[...] = jnp.zeros_like(t_out)

    @pl.loop(0, nb)
    def _(i):
        weight = occ_row(i)

        @pl.loop(0, kk, unroll=True)
        def _(k):
            first = jnp.zeros((ext, nz), jnp.float32)
            second = u0[MID, i, k] + v2[i, k]
            for j in range(nb):
                first = first + lpsi[j] * wide(e0[i, j, pl.ds(k, 1), :])
                second = second + psi[MID, j] * wide(e1[i, j, pl.ds(k, 1), :])
            v2[i, k] = second + h[MID, i] * first
            inner = v2[i, k, core, :]
            for n, s in enumerate((MID - 1, MID + 1)):
                t_out[n, k] += weight * psi[s, i, core, :] * h[s, i, core, :] * inner

    def t_copy(n):
        return remote(t_out.at[n], t_in.at[n], t_send.at[n], t_recv.at[n],
                      {"band": b, "xy": at_slab(2 * n - 1)})

    for n in range(2):
        t_copy(n).start()
        sent.append(t_copy(n))

    dens_ref[...] = jnp.zeros_like(dens_ref)

    @pl.loop(0, nb)
    def _(i):
        weight = occ_row(i)

        @pl.loop(0, kk, unroll=True)
        def _(k):
            beside = (h[MID, i] * around(v2[i, k]))[core, :]
            flat = u0[MID, i, k, core, :]
            for j in range(nb):
                flat = flat + psi[MID, j, core, :] * wide(e2[i, j, pl.ds(k, 1), :])
            dens_ref[k, 0] += weight * psi[MID, i, core, :] * (flat + beside)

    part[0:128, :] = jnp.zeros((128, 128), jnp.float32)

    @pl.loop(0, kk, unroll=True)
    def _(k):
        for l in range(kk):
            put(l * kp + k, tri[MID, l, core, :] * dens_ref[k, 0]
                + tri[MID - 1, l, core, :] * t_out[0, k] + tri[MID + 1, l, core, :] * t_out[1, k])

    scale = 1.0 / math.sqrt(nb)
    total(2, kk * kp, scale / cells, ca)
    column = lax.broadcasted_iota(jnp.int32, (kp, 128), 1)
    picked = sum(jnp.where(column == l, ca[l * kp:(l + 1) * kp, :], 0.0) for l in range(kk))
    resp_ref[...] = picked[:kk, :kk]
    for n in range(2):
        t_copy(n).wait_recv()

    @pl.loop(0, kk, unroll=True)
    def _(k):
        dens_ref[k, 0] = scale * (dens_ref[k, 0] + t_in[0, k] + t_in[1, k])

    for copy in sent:
        copy.wait_send()


def local(sizes, orbitals, energies, occupation, potential, trials):
    bands, slabs = sizes
    nd, width, ny, nz = orbitals.shape
    kk = trials.shape[0]
    nb = nd * bands
    ys = ny // bands
    ext = ys + EDGE
    kp, jp = round_up(kk, 8), round_up(nb, 8)
    block, square = nb * nb * kp, nb * nb * jp
    rows_a = 2 * block + square + nb * jp
    rows_b = 3 * block + 2 * square
    rows_c = kk * kp
    padded = [math.prod(message(rows)) for rows in (rows_a, rows_b)]
    groups = reduce_groups(bands, slabs)
    widest = max(across * size for across, size, stride in groups)

    def f32(*shape):
        return pltpu.VMEM(shape, jnp.float32)

    dma = pltpu.SemaphoreType.DMA
    scratch = [
        f32(SLABS, nb, ext, nz), f32(SLABS, kk + 1, ext, nz), f32(bands, nd, ext, nz),
        f32(bands, 16, nz), f32(SLABS, nb, ext, nz), f32(SLABS, nb, kk, ext, nz),
        f32(2, ext, nz), f32(nb, kk, ext, nz), f32(nb, ext, nz),
        f32(nb, nb, ys, nz), f32(2, kk, ys, nz), f32(2, kk, ys, nz),
        f32(max(padded), 128), f32(padded[0], 128), f32(padded[1], 128),
        f32(nb, nb, kp, 128), f32(nb, nb, kp, 128), f32(nb, nb, kp, 128),
        f32(nb, nb, kp, 128), f32(nb, nb, kp, 128),
        [f32(across * size, 8, message(rows)[1]) for rows in (rows_a, rows_b, rows_c)
         for across, size, stride in groups],
        dma((5, bands)), dma((5, bands)), dma((5,)), dma((5,)),
        dma((bands,)), dma((bands,)), dma((2,)), dma((2,)),
        dma((3, len(groups), widest)), dma((3, len(groups), widest)),
    ]
    vmem = pl.BlockSpec(memory_space=pltpu.VMEM)
    smem = pl.BlockSpec(memory_space=pltpu.SMEM)
    return pl.pallas_call(
        functools.partial(kernel, (bands, slabs, nd, kk, ny, nz), groups),
        out_shape=(jax.ShapeDtypeStruct((kk, width, ys, nz), jnp.float32),
                   jax.ShapeDtypeStruct((kk, kk), jnp.float32)),
        in_specs=[vmem, smem, smem, vmem, vmem],
        out_specs=(vmem, vmem),
        scratch_shapes=scratch,
        compiler_params=pltpu.CompilerParams(collective_id=0, has_side_effects=True,
                                             vmem_limit_bytes=56 * 1024 * 1024),
    )(orbitals, energies, occupation, potential, trials)


def solution(mesh):
    in_specs = (
        P("band", "xy", None, None),
        P("band"),
        P("band"),
        P("xy", None, None),
        P(None, "xy", None, None),
    )
    out_specs = (P(None, "xy", "band", None), P())
    sizes = (mesh.shape["band"], mesh.shape["xy"])
    return jax.shard_map(functools.partial(local, sizes), mesh=mesh, in_specs=in_specs,
                         out_specs=out_specs, check_vma=False)
```

```python
import functools
import math

import jax
import jax.numpy as jnp
from jax import lax
from jax.experimental import pallas as pl
from jax.experimental.pallas import tpu as pltpu
from jax.sharding import PartitionSpec as P

ITERS = 3
REACH = 2
SLABS = 2 * REACH + 1
MID = REACH
EDGE = 8
MIDDLE, PARTNER, NEAR, FAR, PASSED = range(5)
HIGHEST = lax.Precision.HIGHEST


def round_up(value, unit):
    return -(-value // unit) * unit


def reduce_groups(bands, slabs):
    groups = []
    stride = 1
    while stride < slabs:
        size = 4 if (slabs // stride) % 4 == 0 else slabs // stride
        groups.append((1 if groups else bands, size, stride))
        stride *= size
    return groups


def message(rows):
    lines = min(8, -(-rows // 128))
    return lines, round_up(-(-rows // lines), 128)


def kernel(dims, groups, orb_ref, energy_ref, occ_ref, pot_ref, trial_ref, dens_ref, resp_ref,
           psi, tri, psi_out, meta, h, u0, v1, v2, lpsi, a_buf, t_out, t_in,
           part, ca, cb, c0f, cf, e0, e1, e2, reds,
           psi_send, psi_recv, tri_send, tri_recv, meta_send, meta_recv, t_send, t_recv,
           red_send, red_recv):
    bands, slabs, nd, kk, ny, nz = dims
    nb = nd * bands
    ys = ny // bands
    ext = ys + EDGE
    kp, jp = round_up(kk, 8), round_up(nb, 8)
    cells = slabs * ny * nz
    b, p = lax.axis_index("band"), lax.axis_index("xy")

    out = 2 * lax.rem(p, 2) - 1

    def at_band(r):
        return lax.rem(b + (r + bands), bands)

    def at_slab(d):
        return lax.rem(p + (d + slabs), slabs)

    def group_size(g):
        return groups[g][0] * groups[g][1]

    def group_rank(g):
        across, size, stride = groups[g]
        rank = lax.rem(p // stride, size)
        return rank + b * size if across > 1 else rank

    def group_peer(g, q):
        across, size, stride = groups[g]
        peer = lax.rem(group_rank(g) + q, group_size(g))
        step = (lax.rem(peer, size) - lax.rem(p // stride, size)) * stride
        return {"band": peer // size if across > 1 else b, "xy": p + step}

    barrier = pltpu.get_barrier_semaphore()
    count = 0
    for d in range(-REACH, REACH + 1):
        for r in range(bands):
            if d or r:
                pl.semaphore_signal(barrier, inc=1, device_id={"band": at_band(r), "xy": at_slab(d)},
                                    device_id_type=pl.DeviceIdType.MESH)
                count += 1
    for g in range(len(groups)):
        for q in range(1, group_size(g)):
            pl.semaphore_signal(barrier, inc=1, device_id=group_peer(g, q),
                                device_id_type=pl.DeviceIdType.MESH)
            count += 1

    def fill(dst, row_band, src):
        first = pl.multiple_of(row_band * ys, 8)
        low = pl.multiple_of(lax.rem(first + (ny - EDGE), ny), 8)
        high = pl.multiple_of(lax.rem(first + ys, ny), 8)
        dst[0:ys, :] = src[pl.ds(first, ys), :]
        dst[ys:ext, :] = jnp.where(lax.broadcasted_iota(jnp.int32, (EDGE, nz), 0) < EDGE // 2,
                                   src[pl.ds(high, EDGE), :], src[pl.ds(low, EDGE), :])

    own = pl.ds(b * nd, nd)
    for l in range(nd):
        fill(psi.at[MID, b * nd + l], b, orb_ref.at[l, 0])
        for r in range(1, bands):
            fill(psi_out.at[r, l], at_band(r), orb_ref.at[l, 0])
    for k in range(kk):
        fill(tri.at[MID, k], b, trial_ref.at[k, 0])
    fill(tri.at[MID, kk], b, pot_ref.at[0])
    for l in range(nd):
        meta[b, l:l + 1, :] = jnp.full((1, nz), energy_ref[l], jnp.float32)
        meta[b, 8 + l:9 + l, :] = jnp.full((1, nz), occ_ref[l].astype(jnp.float32), jnp.float32)

    pl.semaphore_wait(barrier, count)

    def remote(src, dst, send, recv, device):
        return pltpu.make_async_remote_copy(src_ref=src, dst_ref=dst, send_sem=send, recv_sem=recv,
                                            device_id=device, device_id_type=pl.DeviceIdType.MESH)

    def meta_copy(r, from_band):
        return remote(meta.at[b], meta.at[from_band], meta_send.at[r], meta_recv.at[r],
                      {"band": at_band(r), "xy": p})

    def place(role):
        return {MIDDLE: (0, MID), PARTNER: (-out, MID + out), NEAR: (out, MID - out),
                FAR: (-2 * out, MID + 2 * out), PASSED: (-out, MID + 2 * out)}[role]

    def psi_copy(role, r, first, count):
        d, slot = place(role)
        if role == PASSED:
            src = psi.at[MID + out, :]
        elif r == 0:
            src = psi.at[MID, own]
        elif role == MIDDLE:
            src = psi_out.at[r]
        else:
            src = psi_out.at[r, :]
        dst = psi.at[slot, pl.ds(first, count)]
        if role != MIDDLE:
            dst = psi.at[slot, pl.ds(first, count)]
        return remote(src, dst, psi_send.at[role, r], psi_recv.at[role, r],
                      {"band": at_band(r), "xy": at_slab(d)})

    def tri_copy(role):
        d, slot = place(role)
        src = tri.at[MID + out if role == PASSED else MID, :]
        return remote(src, tri.at[slot, :], tri_send.at[role], tri_recv.at[role],
                      {"band": b, "xy": at_slab(d)})

    def copies(role):
        if role == PASSED:
            return [psi_copy(role, 0, 0, nb), tri_copy(role)]
        moved = [psi_copy(role, r, b * nd, nd) for r in range(bands) if r or role != MIDDLE]
        return moved if role == MIDDLE else moved + [tri_copy(role)]

    sent = []

    def send(role):
        for copy in copies(role):
            copy.start()
            sent.append(copy)

    def wait(role):
        if role == PASSED:
            for copy in copies(role):
                copy.wait_recv()
            return
        for r in range(bands):
            if r or role != MIDDLE:
                psi_copy(role, r, at_band(-r) * nd, nd).wait_recv()
        if role != MIDDLE:
            tri_copy(role).wait_recv()

    for r in range(1, bands):
        meta_copy(r, b).start()
        sent.append(meta_copy(r, b))
    send(MIDDLE)
    send(PARTNER)
    send(NEAR)

    lanes = lax.broadcasted_iota(jnp.int32, (ext, nz), 1)

    def around(c):
        return (pltpu.roll(c, 1, 0) + pltpu.roll(c, ext - 1, 0)
                + jnp.where(lanes == 0, 0.0, pltpu.roll(c, 1, 1))
                + jnp.where(lanes == nz - 1, 0.0, pltpu.roll(c, nz - 1, 1)))

    core = slice(0, ys)

    def put(row, value):
        folded = sum(value[:, z:z + 128] for z in range(0, nz, 128))
        part[pl.ds(row, 1), :] = jnp.sum(folded, axis=0, keepdims=True)

    def total(which, rows, scale, dst):
        count, length = message(rows)
        lines = lax.broadcasted_iota(jnp.int32, (8, 128), 0)
        y = jnp.zeros((8, length), jnp.float32)
        for line in range(count):
            y = y + lax.dot_general(jnp.where(lines == line, 1.0, 0.0),
                                    part[line * length:(line + 1) * length, :],
                                    (((1,), (1,)), ((), ())), precision=HIGHEST,
                                    preferred_element_type=jnp.float32)
        for g in range(len(groups)):
            rank, size = group_rank(g), group_size(g)
            buf = reds[which * len(groups) + g]
            buf[rank, :, :] = y

            def hop(q, slot):
                return remote(buf.at[rank], buf.at[slot], red_send.at[which, g, q],
                              red_recv.at[which, g, q], group_peer(g, q))

            hops = [hop(q, rank) for q in range(1, size)]
            for copy in hops:
                copy.start()
            for q in range(1, size):
                hop(q, lax.rem(rank + (size - q), size)).wait_recv()
            y = buf[0]
            for slot in range(1, size):
                y = y + buf[slot]
            sent.extend(hops)
        for line in range(count):
            dst[line * length:(line + 1) * length, :] = lax.dot_general(
                y, jnp.where(lines == line, scale, 0.0), (((0,), (0,)), ((), ())),
                precision=HIGHEST, preferred_element_type=jnp.float32)

    def wide(row):
        return jnp.concatenate([row] * (nz // 128), axis=1)

    def energy_row(i):
        return meta[i // nd, pl.ds(i % nd, 1), :]

    def occ_row(i):
        return meta[i // nd, pl.ds(8 + i % nd, 1), :]

    def fill_h(s):
        @pl.loop(0, nb)
        def _(i):
            h[s, i] = 0.5 / (3.0 + tri[s, kk] - energy_row(i))

    for r in range(1, bands):
        meta_copy(r, at_band(-r)).wait_recv()
    wait(MIDDLE)
    fill_h(MID)
    block = nb * nb * kp
    square = nb * nb * jp
    part[...] = jnp.zeros_like(part)

    @pl.loop(0, nb)
    def _(i):
        mine = psi[MID, i, core, :]
        inv = 2.0 * h[MID, i, core, :]

        @pl.loop(0, nb, unroll=min(nb, 2))
        def _(j):
            other = psi[MID, j, core, :]
            pair = mine * other
            for k in range(kk):
                both = pair * tri[MID, k, core, :]
                put((i * nb + j) * kp + k, both)
                put(block + (i * nb + j) * kp + k, both * inv)
            weighted = other * inv
            for m in range(nb):
                put(2 * block + (i * nb + j) * jp + m, weighted * psi[MID, m, core, :])
            put(2 * block + square + i * jp + j, pair)

    size_a = 2 * block + square + nb * jp
    total(0, size_a, 1.0 / cells, ca)
    send(FAR)

    def tile(ref, base, i, j, unit):
        return ref[pl.ds(pl.multiple_of(base + (i * nb + j) * unit, 8), 8), :]

    def apply(ref, base, i, j, vectors):
        return sum(ref[pl.ds(base + (i * nb + j) * jp + m, 1), :] * vectors[m] for m in range(nb))

    def gram(j, vectors):
        base = 2 * block + square + j * jp
        return sum(ca[base + m:base + m + 1, :] * vectors[m] for m in range(nb))

    @pl.loop(0, nb)
    def _(i):
        c0 = [tile(ca, 0, i, j, kp) for j in range(nb)]
        for j in range(nb):
            cf[i, j] = apply(ca, 2 * block, i, j, c0) - tile(ca, block, i, j, kp)
            c0f[i, j] = c0[j]

    chunk = 24 if ext % 24 == 0 else 8

    def fill_u0(s):
        @pl.loop(0, nb)
        def _(i):
            @pl.loop(0, ext // chunk)
            def _(c):
                rows = pl.ds(pl.multiple_of(c * chunk, 8), chunk)
                mine = psi[s, i, rows, :]
                inv = 2.0 * h[s, i, rows, :]
                for k in range(kk):
                    first = -(tri[s, k, rows, :] * mine)
                    second = jnp.zeros_like(first)
                    for j in range(nb):
                        field = psi[s, j, rows, :]
                        first = first + field * wide(c0f[i, j, k:k + 1, :])
                        second = second + field * wide(cf[i, j, k:k + 1, :])
                    u0[s, i, k, rows, :] = inv * first - second

    fill_u0(MID)
    wait(PARTNER)
    fill_h(MID - out)
    fill_u0(MID - out)
    wait(NEAR)
    send(PASSED)
    fill_h(MID + out)
    fill_u0(MID + out)

    part[...] = jnp.zeros_like(part)

    @pl.loop(0, nb)
    def _(j):
        lpsi[j] = psi[MID - 1, j] + psi[MID + 1, j] + around(psi[MID, j])

    @pl.loop(0, nb)
    def _(i):
        @pl.loop(0, nb, unroll=min(nb, 4))
        def _(j):
            a_buf[i, j] = (h[MID - 1, i] * psi[MID - 1, j] + h[MID + 1, i] * psi[MID + 1, j]
                           + around(h[MID, i] * psi[MID, j]))[core, :]

        @pl.loop(0, nb, unroll=min(nb, 4))
        def _(m):
            seen = h[MID, i, core, :] * lpsi[m, core, :]
            for j in range(nb):
                row = (i * nb + j) * jp + m
                put(3 * block + row, psi[MID, j, core, :] * seen)
                put(3 * block + square + row, a_buf[i, j] * seen)

        @pl.loop(0, kk, unroll=True)
        def _(k):
            v2[i, k] = h[MID, i] * (u0[MID - 1, i, k] + u0[MID + 1, i, k] + around(u0[MID, i, k]))
            first = v2[i, k, core, :]
            for j in range(nb):
                put((i * nb + j) * kp + k, psi[MID, j, core, :] * first)

    wait(FAR)
    fill_h(MID + 2 * out)
    fill_u0(MID + 2 * out)
    wait(PASSED)
    fill_h(MID - 2 * out)
    fill_u0(MID - 2 * out)

    @pl.loop(0, nb)
    def _(i):
        @pl.loop(0, kk, unroll=True)
        def _(k):
            for n, s in enumerate((MID - 1, MID + 1)):
                v1[n] = u0[s, i, k] + h[s, i] * (u0[s - 1, i, k] + u0[s + 1, i, k]
                                                + around(u0[s, i, k]))
            v2[i, k] = h[MID, i] * (v1[0] + v1[1] + around(u0[MID, i, k] + v2[i, k]))
            second = v2[i, k, core, :]
            for j in range(nb):
                row = (i * nb + j) * kp + k
                put(block + row, psi[MID, j, core, :] * second)
                put(2 * block + row, a_buf[i, j] * second)

    size_b = 3 * block + 2 * square
    total(1, size_b, 1.0 / cells, cb)

    @pl.loop(0, nb)
    def _(i):
        once = 3 * block
        twice = 3 * block + square
        start = [cf[i, j] for j in range(nb)]
        mu1 = [tile(cb, 0, i, j, kp) for j in range(nb)]
        b0 = [start[j] - gram(j, start) for j in range(nb)]
        x0 = [b0[j] - mu1[j] for j in range(nb)]
        m1 = [tile(cb, block, i, j, kp) + apply(cb, once, i, j, x0) for j in range(nb)]
        x1 = [b0[j] + mu1[j] + gram(j, x0) - m1[j] for j in range(nb)]
        m2 = [mu1[j] + tile(cb, 2 * block, i, j, kp) + apply(cb, twice, i, j, x0)
              + apply(cb, once, i, j, x1) for j in range(nb)]
        for j in range(nb):
            e0[i, j] = x0[j]
            e1[i, j] = x1[j]
            e2[i, j] = b0[j] + m1[j] + gram(j, x1) - m2[j]

    t_out[...] = jnp.zeros_like(t_out)

    @pl.loop(0, nb)
    def _(i):
        weight = occ_row(i)

        @pl.loop(0, ext // chunk)
        def _(c):
            rows = pl.ds(pl.multiple_of(c * chunk, 8), chunk)
            half = h[MID, i, rows, :]
            for k in range(kk):
                first = jnp.zeros((chunk, nz), jnp.float32)
                second = u0[MID, i, k, rows, :] + v2[i, k, rows, :]
                for j in range(nb):
                    first = first + lpsi[j, rows, :] * wide(e0[i, j, k:k + 1, :])
                    second = second + psi[MID, j, rows, :] * wide(e1[i, j, k:k + 1, :])
                v2[i, k, rows, :] = second + half * first

        for n, s in enumerate((MID - 1, MID + 1)):
            factor = weight * psi[s, i, core, :] * h[s, i, core, :]
            for k in range(kk):
                t_out[n, k] += factor * v2[i, k, core, :]

    def t_copy(n):
        return remote(t_out.at[n], t_in.at[n], t_send.at[n], t_recv.at[n],
                      {"band": b, "xy": at_slab(2 * n - 1)})

    for n in range(2):
        t_copy(n).start()
        sent.append(t_copy(n))

    dens_ref[...] = jnp.zeros_like(dens_ref)

    @pl.loop(0, nb)
    def _(i):
        weight = occ_row(i)

        @pl.loop(0, kk, unroll=True)
        def _(k):
            beside = (h[MID, i] * around(v2[i, k]))[core, :]
            flat = u0[MID, i, k, core, :]
            for j in range(nb):
                flat = flat + psi[MID, j, core, :] * wide(e2[i, j, pl.ds(k, 1), :])
            dens_ref[k, 0] += weight * psi[MID, i, core, :] * (flat + beside)

    part[0:128, :] = jnp.zeros((128, 128), jnp.float32)

    @pl.loop(0, kk, unroll=True)
    def _(k):
        for l in range(kk):
            put(l * kp + k, tri[MID, l, core, :] * dens_ref[k, 0]
                + tri[MID - 1, l, core, :] * t_out[0, k] + tri[MID + 1, l, core, :] * t_out[1, k])

    scale = 1.0 / math.sqrt(nb)
    total(2, kk * kp, scale / cells, ca)
    column = lax.broadcasted_iota(jnp.int32, (kp, 128), 1)
    picked = sum(jnp.where(column == l, ca[l * kp:(l + 1) * kp, :], 0.0) for l in range(kk))
    resp_ref[...] = picked[:kk, :kk]
    for n in range(2):
        t_copy(n).wait_recv()

    @pl.loop(0, kk, unroll=True)
    def _(k):
        dens_ref[k, 0] = scale * (dens_ref[k, 0] + t_in[0, k] + t_in[1, k])

    for copy in sent:
        copy.wait_send()


def local(sizes, orbitals, energies, occupation, potential, trials):
    bands, slabs = sizes
    nd, width, ny, nz = orbitals.shape
    kk = trials.shape[0]
    nb = nd * bands
    ys = ny // bands
    ext = ys + EDGE
    kp, jp = round_up(kk, 8), round_up(nb, 8)
    block, square = nb * nb * kp, nb * nb * jp
    rows_a = 2 * block + square + nb * jp
    rows_b = 3 * block + 2 * square
    rows_c = kk * kp
    padded = [math.prod(message(rows)) for rows in (rows_a, rows_b)]
    groups = reduce_groups(bands, slabs)
    widest = max(across * size for across, size, stride in groups)

    def f32(*shape):
        return pltpu.VMEM(shape, jnp.float32)

    dma = pltpu.SemaphoreType.DMA
    scratch = [
        f32(SLABS, nb, ext, nz), f32(SLABS, kk + 1, ext, nz), f32(bands, nd, ext, nz),
        f32(bands, 16, nz), f32(SLABS, nb, ext, nz), f32(SLABS, nb, kk, ext, nz),
        f32(2, ext, nz), f32(nb, kk, ext, nz), f32(nb, ext, nz),
        f32(nb, nb, ys, nz), f32(2, kk, ys, nz), f32(2, kk, ys, nz),
        f32(max(padded), 128), f32(padded[0], 128), f32(padded[1], 128),
        f32(nb, nb, kp, 128), f32(nb, nb, kp, 128), f32(nb, nb, kp, 128),
        f32(nb, nb, kp, 128), f32(nb, nb, kp, 128),
        [f32(across * size, 8, message(rows)[1]) for rows in (rows_a, rows_b, rows_c)
         for across, size, stride in groups],
        dma((5, bands)), dma((5, bands)), dma((5,)), dma((5,)),
        dma((bands,)), dma((bands,)), dma((2,)), dma((2,)),
        dma((3, len(groups), widest)), dma((3, len(groups), widest)),
    ]
    vmem = pl.BlockSpec(memory_space=pltpu.VMEM)
    smem = pl.BlockSpec(memory_space=pltpu.SMEM)
    return pl.pallas_call(
        functools.partial(kernel, (bands, slabs, nd, kk, ny, nz), groups),
        out_shape=(jax.ShapeDtypeStruct((kk, width, ys, nz), jnp.float32),
                   jax.ShapeDtypeStruct((kk, kk), jnp.float32)),
        in_specs=[vmem, smem, smem, vmem, vmem],
        out_specs=(vmem, vmem),
        scratch_shapes=scratch,
        compiler_params=pltpu.CompilerParams(collective_id=0, has_side_effects=True,
                                             vmem_limit_bytes=56 * 1024 * 1024),
    )(orbitals, energies, occupation, potential, trials)


def solution(mesh):
    in_specs = (
        P("band", "xy", None, None),
        P("band"),
        P("band"),
        P("xy", None, None),
        P(None, "xy", None, None),
    )
    out_specs = (P(None, "xy", "band", None), P())
    sizes = (mesh.shape["band"], mesh.shape["xy"])
    return jax.shard_map(functools.partial(local, sizes), mesh=mesh, in_specs=in_specs,
                         out_specs=out_specs, check_vma=False)
```

```python
import functools
import math

import jax
import jax.numpy as jnp
from jax import lax
from jax.experimental import pallas as pl
from jax.experimental.pallas import tpu as pltpu
from jax.sharding import PartitionSpec as P

ITERS = 3
REACH = 2
SLABS = 2 * REACH + 1
MID = REACH
EDGE = 8
MIDDLE, PARTNER, NEAR, FAR, PASSED = range(5)
HIGHEST = lax.Precision.HIGHEST


def round_up(value, unit):
    return -(-value // unit) * unit


def reduce_groups(bands, slabs):
    groups = []
    stride = 1
    while stride < slabs:
        size = 4 if (slabs // stride) % 4 == 0 else slabs // stride
        groups.append((1 if groups else bands, size, stride))
        stride *= size
    return groups


def message(rows):
    lines = min(8, -(-rows // 128))
    return lines, round_up(-(-rows // lines), 128)


def kernel(dims, groups, orb_ref, energy_ref, occ_ref, pot_ref, trial_ref, dens_ref, resp_ref,
           psi, tri, psi_out, meta, h, u0, v1, v2, lpsi, a_buf, t_out, t_in,
           part, ca, cb, c0f, cf, e0, e1, e2, reds,
           psi_send, psi_recv, tri_send, tri_recv, meta_send, meta_recv, t_send, t_recv,
           red_send, red_recv):
    bands, slabs, nd, kk, ny, nz = dims
    nb = nd * bands
    ys = ny // bands
    ext = ys + EDGE
    kp, jp = round_up(kk, 8), round_up(nb, 8)
    cells = slabs * ny * nz
    b, p = lax.axis_index("band"), lax.axis_index("xy")

    out = 2 * lax.rem(p, 2) - 1

    def at_band(r):
        return lax.rem(b + (r + bands), bands)

    def at_slab(d):
        return lax.rem(p + (d + slabs), slabs)

    def group_size(g):
        return groups[g][0] * groups[g][1]

    def group_rank(g):
        across, size, stride = groups[g]
        rank = lax.rem(p // stride, size)
        return rank + b * size if across > 1 else rank

    def group_peer(g, q):
        across, size, stride = groups[g]
        peer = lax.rem(group_rank(g) + q, group_size(g))
        step = (lax.rem(peer, size) - lax.rem(p // stride, size)) * stride
        return {"band": peer // size if across > 1 else b, "xy": p + step}

    barrier = pltpu.get_barrier_semaphore()
    count = 0
    for d in range(-REACH, REACH + 1):
        for r in range(bands):
            if d or r:
                pl.semaphore_signal(barrier, inc=1, device_id={"band": at_band(r), "xy": at_slab(d)},
                                    device_id_type=pl.DeviceIdType.MESH)
                count += 1
    for g in range(len(groups)):
        for q in range(1, group_size(g)):
            pl.semaphore_signal(barrier, inc=1, device_id=group_peer(g, q),
                                device_id_type=pl.DeviceIdType.MESH)
            count += 1

    def fill(dst, row_band, src):
        first = pl.multiple_of(row_band * ys, 8)
        low = pl.multiple_of(lax.rem(first + (ny - EDGE), ny), 8)
        high = pl.multiple_of(lax.rem(first + ys, ny), 8)
        dst[0:ys, :] = src[pl.ds(first, ys), :]
        dst[ys:ext, :] = jnp.where(lax.broadcasted_iota(jnp.int32, (EDGE, nz), 0) < EDGE // 2,
                                   src[pl.ds(high, EDGE), :], src[pl.ds(low, EDGE), :])

    own = pl.ds(b * nd, nd)
    for l in range(nd):
        fill(psi.at[MID, b * nd + l], b, orb_ref.at[l, 0])
        for r in range(1, bands):
            fill(psi_out.at[r, l], at_band(r), orb_ref.at[l, 0])
    for k in range(kk):
        fill(tri.at[MID, k], b, trial_ref.at[k, 0])
    fill(tri.at[MID, kk], b, pot_ref.at[0])
    for l in range(nd):
        meta[b, l:l + 1, :] = jnp.full((1, nz), energy_ref[l], jnp.float32)
        meta[b, 8 + l:9 + l, :] = jnp.full((1, nz), occ_ref[l].astype(jnp.float32), jnp.float32)

    pl.semaphore_wait(barrier, count)

    def remote(src, dst, send, recv, device):
        return pltpu.make_async_remote_copy(src_ref=src, dst_ref=dst, send_sem=send, recv_sem=recv,
                                            device_id=device, device_id_type=pl.DeviceIdType.MESH)

    def meta_copy(r, from_band):
        return remote(meta.at[b], meta.at[from_band], meta_send.at[r], meta_recv.at[r],
                      {"band": at_band(r), "xy": p})

    def place(role):
        return {MIDDLE: (0, MID), PARTNER: (-out, MID + out), NEAR: (out, MID - out),
                FAR: (-2 * out, MID + 2 * out), PASSED: (-out, MID + 2 * out)}[role]

    def psi_copy(role, r, first, count):
        d, slot = place(role)
        if role == PASSED:
            src = psi.at[MID + out, :]
        elif r == 0:
            src = psi.at[MID, own]
        elif role == MIDDLE:
            src = psi_out.at[r]
        else:
            src = psi_out.at[r, :]
        dst = psi.at[slot, pl.ds(first, count)]
        if role != MIDDLE:
            dst = psi.at[slot, pl.ds(first, count)]
        return remote(src, dst, psi_send.at[role, r], psi_recv.at[role, r],
                      {"band": at_band(r), "xy": at_slab(d)})

    def tri_copy(role):
        d, slot = place(role)
        src = tri.at[MID + out if role == PASSED else MID, :]
        return remote(src, tri.at[slot, :], tri_send.at[role], tri_recv.at[role],
                      {"band": b, "xy": at_slab(d)})

    def copies(role):
        if role == PASSED:
            return [psi_copy(role, 0, 0, nb), tri_copy(role)]
        moved = [psi_copy(role, r, b * nd, nd) for r in range(bands) if r or role != MIDDLE]
        return moved if role == MIDDLE else moved + [tri_copy(role)]

    sent = []

    def send(role):
        for copy in copies(role):
            copy.start()
            sent.append(copy)

    def wait(role):
        if role == PASSED:
            for copy in copies(role):
                copy.wait_recv()
            return
        for r in range(bands):
            if r or role != MIDDLE:
                psi_copy(role, r, at_band(-r) * nd, nd).wait_recv()
        if role != MIDDLE:
            tri_copy(role).wait_recv()

    for r in range(1, bands):
        meta_copy(r, b).start()
        sent.append(meta_copy(r, b))
    send(MIDDLE)
    send(PARTNER)
    send(NEAR)

    lanes = lax.broadcasted_iota(jnp.int32, (ext, nz), 1)

    def around(c):
        return (pltpu.roll(c, 1, 0) + pltpu.roll(c, ext - 1, 0)
                + jnp.where(lanes == 0, 0.0, pltpu.roll(c, 1, 1))
                + jnp.where(lanes == nz - 1, 0.0, pltpu.roll(c, nz - 1, 1)))

    core = slice(0, ys)

    def put(row, value):
        folded = sum(value[:, z:z + 128] for z in range(0, nz, 128))
        part[pl.ds(row, 1), :] = jnp.sum(folded, axis=0, keepdims=True)

    def total(which, rows, scale, dst, beside=None):
        count, length = message(rows)
        lines = lax.broadcasted_iota(jnp.int32, (8, 128), 0)
        y = jnp.zeros((8, length), jnp.float32)
        for line in range(count):
            y = y + lax.dot_general(jnp.where(lines == line, 1.0, 0.0),
                                    part[line * length:(line + 1) * length, :],
                                    (((1,), (1,)), ((), ())), precision=HIGHEST,
                                    preferred_element_type=jnp.float32)
        for g in range(len(groups)):
            rank, size = group_rank(g), group_size(g)
            buf = reds[which * len(groups) + g]
            buf[rank, :, :] = y

            def hop(q, slot):
                return remote(buf.at[rank], buf.at[slot], red_send.at[which, g, q],
                              red_recv.at[which, g, q], group_peer(g, q))

            hops = [hop(q, rank) for q in range(1, size)]
            for copy in hops:
                copy.start()
            if beside and g == len(groups) - 1:
                beside()
            for q in range(1, size):
                hop(q, lax.rem(rank + (size - q), size)).wait_recv()
            y = buf[0]
            for slot in range(1, size):
                y = y + buf[slot]
            sent.extend(hops)
        for line in range(count):
            dst[line * length:(line + 1) * length, :] = lax.dot_general(
                y, jnp.where(lines == line, scale, 0.0), (((0,), (0,)), ((), ())),
                precision=HIGHEST, preferred_element_type=jnp.float32)

    def wide(row):
        return jnp.concatenate([row] * (nz // 128), axis=1)

    def energy_row(i):
        return meta[i // nd, pl.ds(i % nd, 1), :]

    def occ_row(i):
        return meta[i // nd, pl.ds(8 + i % nd, 1), :]

    def fill_h(s):
        @pl.loop(0, nb)
        def _(i):
            h[s, i] = 0.5 / (3.0 + tri[s, kk] - energy_row(i))

    for r in range(1, bands):
        meta_copy(r, at_band(-r)).wait_recv()
    wait(MIDDLE)
    fill_h(MID)
    block = nb * nb * kp
    square = nb * nb * jp
    part[...] = jnp.zeros_like(part)

    @pl.loop(0, nb)
    def _(i):
        mine = psi[MID, i, core, :]
        inv = 2.0 * h[MID, i, core, :]

        @pl.loop(0, nb, unroll=min(nb, 2))
        def _(j):
            other = psi[MID, j, core, :]
            pair = mine * other
            for k in range(kk):
                both = pair * tri[MID, k, core, :]
                put((i * nb + j) * kp + k, both)
                put(block + (i * nb + j) * kp + k, both * inv)
            weighted = other * inv
            for m in range(nb):
                put(2 * block + (i * nb + j) * jp + m, weighted * psi[MID, m, core, :])
            put(2 * block + square + i * jp + j, pair)

    size_a = 2 * block + square + nb * jp
    total(0, size_a, 1.0 / cells, ca, lambda: send(FAR))

    def tile(ref, base, i, j, unit):
        return ref[pl.ds(pl.multiple_of(base + (i * nb + j) * unit, 8), 8), :]

    def apply(ref, base, i, j, vectors):
        return sum(ref[pl.ds(base + (i * nb + j) * jp + m, 1), :] * vectors[m] for m in range(nb))

    def gram(j, vectors):
        base = 2 * block + square + j * jp
        return sum(ca[base + m:base + m + 1, :] * vectors[m] for m in range(nb))

    @pl.loop(0, nb)
    def _(i):
        c0 = [tile(ca, 0, i, j, kp) for j in range(nb)]
        for j in range(nb):
            cf[i, j] = apply(ca, 2 * block, i, j, c0) - tile(ca, block, i, j, kp)
            c0f[i, j] = c0[j]

    chunk = 24 if ext % 24 == 0 else 8

    def fill_u0(s):
        @pl.loop(0, nb)
        def _(i):
            @pl.loop(0, ext // chunk)
            def _(c):
                rows = pl.ds(pl.multiple_of(c * chunk, 8), chunk)
                mine = psi[s, i, rows, :]
                inv = 2.0 * h[s, i, rows, :]
                for k in range(kk):
                    first = -(tri[s, k, rows, :] * mine)
                    second = jnp.zeros_like(first)
                    for j in range(nb):
                        field = psi[s, j, rows, :]
                        first = first + field * wide(c0f[i, j, k:k + 1, :])
                        second = second + field * wide(cf[i, j, k:k + 1, :])
                    u0[s, i, k, rows, :] = inv * first - second

    fill_u0(MID)
    wait(PARTNER)
    fill_h(MID - out)
    fill_u0(MID - out)
    wait(NEAR)
    send(PASSED)
    fill_h(MID + out)
    fill_u0(MID + out)

    part[...] = jnp.zeros_like(part)

    @pl.loop(0, nb)
    def _(j):
        lpsi[j] = psi[MID - 1, j] + psi[MID + 1, j] + around(psi[MID, j])

    @pl.loop(0, nb)
    def _(i):
        @pl.loop(0, nb, unroll=min(nb, 4))
        def _(j):
            a_buf[i, j] = (h[MID - 1, i] * psi[MID - 1, j] + h[MID + 1, i] * psi[MID + 1, j]
                           + around(h[MID, i] * psi[MID, j]))[core, :]

        @pl.loop(0, nb, unroll=min(nb, 4))
        def _(m):
            seen = h[MID, i, core, :] * lpsi[m, core, :]
            for j in range(nb):
                row = (i * nb + j) * jp + m
                put(3 * block + row, psi[MID, j, core, :] * seen)
                put(3 * block + square + row, a_buf[i, j] * seen)

        @pl.loop(0, kk, unroll=True)
        def _(k):
            v2[i, k] = h[MID, i] * (u0[MID - 1, i, k] + u0[MID + 1, i, k] + around(u0[MID, i, k]))
            first = v2[i, k, core, :]
            for j in range(nb):
                put((i * nb + j) * kp + k, psi[MID, j, core, :] * first)

    wait(FAR)
    fill_h(MID + 2 * out)
    fill_u0(MID + 2 * out)
    wait(PASSED)
    fill_h(MID - 2 * out)
    fill_u0(MID - 2 * out)

    @pl.loop(0, nb)
    def _(i):
        @pl.loop(0, kk, unroll=True)
        def _(k):
            for n, s in enumerate((MID - 1, MID + 1)):
                v1[n] = u0[s, i, k] + h[s, i] * (u0[s - 1, i, k] + u0[s + 1, i, k]
                                                + around(u0[s, i, k]))
            v2[i, k] = h[MID, i] * (v1[0] + v1[1] + around(u0[MID, i, k] + v2[i, k]))
            second = v2[i, k, core, :]
            for j in range(nb):
                row = (i * nb + j) * kp + k
                put(block + row, psi[MID, j, core, :] * second)
                put(2 * block + row, a_buf[i, j] * second)

    size_b = 3 * block + 2 * square
    total(1, size_b, 1.0 / cells, cb)

    @pl.loop(0, nb)
    def _(i):
        once = 3 * block
        twice = 3 * block + square
        start = [cf[i, j] for j in range(nb)]
        mu1 = [tile(cb, 0, i, j, kp) for j in range(nb)]
        b0 = [start[j] - gram(j, start) for j in range(nb)]
        x0 = [b0[j] - mu1[j] for j in range(nb)]
        m1 = [tile(cb, block, i, j, kp) + apply(cb, once, i, j, x0) for j in range(nb)]
        x1 = [b0[j] + mu1[j] + gram(j, x0) - m1[j] for j in range(nb)]
        m2 = [mu1[j] + tile(cb, 2 * block, i, j, kp) + apply(cb, twice, i, j, x0)
              + apply(cb, once, i, j, x1) for j in range(nb)]
        for j in range(nb):
            e0[i, j] = x0[j]
            e1[i, j] = x1[j]
            e2[i, j] = b0[j] + m1[j] + gram(j, x1) - m2[j]

    t_out[...] = jnp.zeros_like(t_out)

    @pl.loop(0, nb)
    def _(i):
        weight = occ_row(i)

        @pl.loop(0, ext // chunk)
        def _(c):
            rows = pl.ds(pl.multiple_of(c * chunk, 8), chunk)
            half = h[MID, i, rows, :]
            for k in range(kk):
                first = jnp.zeros((chunk, nz), jnp.float32)
                second = u0[MID, i, k, rows, :] + v2[i, k, rows, :]
                for j in range(nb):
                    first = first + lpsi[j, rows, :] * wide(e0[i, j, k:k + 1, :])
                    second = second + psi[MID, j, rows, :] * wide(e1[i, j, k:k + 1, :])
                v2[i, k, rows, :] = second + half * first

        for n, s in enumerate((MID - 1, MID + 1)):
            factor = weight * psi[s, i, core, :] * h[s, i, core, :]
            for k in range(kk):
                t_out[n, k] += factor * v2[i, k, core, :]

    def t_copy(n):
        return remote(t_out.at[n], t_in.at[n], t_send.at[n], t_recv.at[n],
                      {"band": b, "xy": at_slab(2 * n - 1)})

    for n in range(2):
        t_copy(n).start()
        sent.append(t_copy(n))

    dens_ref[...] = jnp.zeros_like(dens_ref)

    @pl.loop(0, nb)
    def _(i):
        weight = occ_row(i)

        @pl.loop(0, kk, unroll=True)
        def _(k):
            beside = (h[MID, i] * around(v2[i, k]))[core, :]
            flat = u0[MID, i, k, core, :]
            for j in range(nb):
                flat = flat + psi[MID, j, core, :] * wide(e2[i, j, pl.ds(k, 1), :])
            dens_ref[k, 0] += weight * psi[MID, i, core, :] * (flat + beside)

    part[0:128, :] = jnp.zeros((128, 128), jnp.float32)

    @pl.loop(0, kk, unroll=True)
    def _(k):
        for l in range(kk):
            put(l * kp + k, tri[MID, l, core, :] * dens_ref[k, 0]
                + tri[MID - 1, l, core, :] * t_out[0, k] + tri[MID + 1, l, core, :] * t_out[1, k])

    scale = 1.0 / math.sqrt(nb)
    total(2, kk * kp, scale / cells, ca)
    column = lax.broadcasted_iota(jnp.int32, (kp, 128), 1)
    picked = sum(jnp.where(column == l, ca[l * kp:(l + 1) * kp, :], 0.0) for l in range(kk))
    resp_ref[...] = picked[:kk, :kk]
    for n in range(2):
        t_copy(n).wait_recv()

    @pl.loop(0, kk, unroll=True)
    def _(k):
        dens_ref[k, 0] += t_in[0, k] + t_in[1, k]

    for copy in sent:
        copy.wait_send()


def local(sizes, orbitals, energies, occupation, potential, trials):
    bands, slabs = sizes
    nd, width, ny, nz = orbitals.shape
    kk = trials.shape[0]
    nb = nd * bands
    ys = ny // bands
    ext = ys + EDGE
    kp, jp = round_up(kk, 8), round_up(nb, 8)
    block, square = nb * nb * kp, nb * nb * jp
    rows_a = 2 * block + square + nb * jp
    rows_b = 3 * block + 2 * square
    rows_c = kk * kp
    padded = [math.prod(message(rows)) for rows in (rows_a, rows_b)]
    groups = reduce_groups(bands, slabs)
    widest = max(across * size for across, size, stride in groups)

    def f32(*shape):
        return pltpu.VMEM(shape, jnp.float32)

    dma = pltpu.SemaphoreType.DMA
    scratch = [
        f32(SLABS, nb, ext, nz), f32(SLABS, kk + 1, ext, nz), f32(bands, nd, ext, nz),
        f32(bands, 16, nz), f32(SLABS, nb, ext, nz), f32(SLABS, nb, kk, ext, nz),
        f32(2, ext, nz), f32(nb, kk, ext, nz), f32(nb, ext, nz),
        f32(nb, nb, ys, nz), f32(2, kk, ys, nz), f32(2, kk, ys, nz),
        f32(max(padded), 128), f32(padded[0], 128), f32(padded[1], 128),
        f32(nb, nb, kp, 128), f32(nb, nb, kp, 128), f32(nb, nb, kp, 128),
        f32(nb, nb, kp, 128), f32(nb, nb, kp, 128),
        [f32(across * size, 8, message(rows)[1]) for rows in (rows_a, rows_b, rows_c)
         for across, size, stride in groups],
        dma((5, bands)), dma((5, bands)), dma((5,)), dma((5,)),
        dma((bands,)), dma((bands,)), dma((2,)), dma((2,)),
        dma((3, len(groups), widest)), dma((3, len(groups), widest)),
    ]
    vmem = pl.BlockSpec(memory_space=pltpu.VMEM)
    smem = pl.BlockSpec(memory_space=pltpu.SMEM)
    density, response_matrix = pl.pallas_call(
        functools.partial(kernel, (bands, slabs, nd, kk, ny, nz), groups),
        out_shape=(jax.ShapeDtypeStruct((kk, width, ys, nz), jnp.float32),
                   jax.ShapeDtypeStruct((kk, kk), jnp.float32)),
        in_specs=[vmem, smem, smem, vmem, vmem],
        out_specs=(vmem, vmem),
        scratch_shapes=scratch,
        compiler_params=pltpu.CompilerParams(collective_id=0, has_side_effects=True,
                                             vmem_limit_bytes=56 * 1024 * 1024),
    )(orbitals, energies, occupation, potential, trials)
    return density / math.sqrt(nb), response_matrix


def solution(mesh):
    in_specs = (
        P("band", "xy", None, None),
        P("band"),
        P("band"),
        P("xy", None, None),
        P(None, "xy", None, None),
    )
    out_specs = (P(None, "xy", "band", None), P())
    sizes = (mesh.shape["band"], mesh.shape["xy"])
    return jax.shard_map(functools.partial(local, sizes), mesh=mesh, in_specs=in_specs,
                         out_specs=out_specs, check_vma=False)
```
